512 devices in a mesh: tensor: 8 (over y), near: 2 (over z_hi), far: 32 (over z_lo, x, core).
Axes of the slice: x: 4, y: 8, z: 8 (z_hi: 2, z_lo: 4; z = z_hi * 4 + z_lo), core: 2. Of those that a mesh axis runs over, the one named last changes fastest.
Arguments:
- grad_output: bfloat16 [8192, 2304], P(('near', 'far')), may hold values from -6 to 6
- layer_input: bfloat16 [2, 8192, 2304], P(None, ('near', 'far'), 'tensor'), may hold values from -16 to 16
- norm_gain: float32 [2, 2304], replicated, may hold values from 0.5 to 2
- queries: bfloat16 [2, 8192, 2048], P(None, ('near', 'far'), 'tensor'), may hold values from -6 to 6
- keys: bfloat16 [2, 8192, 1024], P(None, ('near', 'far'), 'tensor'), may hold values from -6 to 6
- value_weight: bfloat16 [2, 2304, 1024], P(None, None, 'tensor'), may hold values from -0.125 to 0.125
- output_weight: bfloat16 [2, 2048, 2304], P(None, 'tensor', 'near'), may hold values from -0.125 to 0.125
Outputs:
- grad_input: bfloat16 [8192, 2304], P(('near', 'far'), 'tensor')
- grad_value_weight: float32 [2, 2304, 1024], P(None, ('near', 'far'), 'tensor')
- grad_norm_gain: float32 [2, 2304], P(None, 'tensor')
The draws below stay inside these ranges and needn't reach their ends.
All inputs are finite; a program needn't handle non-finite values.
Results may differ from the reference program's by a relative error of at most 0.023.
Values may be sent and summed in bfloat16 or wider, within the bound.
A program may use at most 64 MiB of HBM per device.

```python
import math
import jax
import jax.numpy as jnp
from jax import lax

D = 2304
HD = 128
KVH_DEV = 1
LAYERS = 2
TOK_DEV = 128
KVH = 8
QH = 16
TOKENS = 8192
N_TENSOR = 8


def spiked(drawn, key, source, target, parts, factor):
    def block_of(position):
        return (jnp.arange(drawn.shape[position]) // (drawn.shape[position] // parts)).reshape((-1,) + (1,) * (drawn.ndim - 1 - position))

    near = jax.random.permutation(key, parts)[block_of(target)]
    other_side = (block_of(target) + parts // 2) % parts
    return jnp.where((block_of(source) == near) | (block_of(source) == other_side), factor * drawn, drawn)


def level_of(stream_key, extent, split, least, largest):
    def one(axis_at, blocks):
        draws = jax.random.uniform(jax.random.fold_in(jax.random.fold_in(stream_key, 6), axis_at), (blocks,), jnp.float32, least / len(split), largest / len(split))
        return jnp.repeat(jnp.exp(draws), extent[axis_at] // blocks).reshape((-1,) + (1,) * (len(extent) - axis_at - 1))

    loudness = one(*split[0])
    for cut in split[1:]:
        loudness = loudness * one(*cut)
    return loudness


def gaussian(rng, shape, width, reach, shards=(), kind=jnp.bfloat16):
    drawn = jax.random.normal(rng, shape, jnp.float32) * width
    if len(shards) > 0:
        drawn = level_of(rng, shape, shards, -0.22, 0.18) * drawn
    return jnp.clip(drawn, min=-reach, max=reach).astype(kind)


def bell_draw_with(key, dims, deviation, limit, pieces, heavy, kind=jnp.bfloat16):
    drawn = deviation * jax.random.normal(key, dims, jnp.float32)
    if pieces:
        drawn = drawn * level_of(key, dims, pieces, -0.22, 0.18)
    return jnp.clip(spiked(drawn, jax.random.fold_in(key, 3), *heavy), -limit, limit).astype(kind)


def setup_inputs(seed: int = 0) -> dict:
    arg_keys = jax.random.split(jax.random.key(seed), 8)
    grad_output = gaussian(arg_keys[0], (TOKENS, D), 1.0, 6.0, ((0, 64),))
    layer_input = bell_draw_with(arg_keys[1], (LAYERS, TOKENS, D), 1.0, 16.0, ((1, 64), (2, 8)), (1, 2, 64, 4.0))
    norm_gain = jnp.clip(jnp.exp(jax.random.uniform(arg_keys[2], (LAYERS, D), jnp.float32, math.log(0.5), math.log(2.0))), 0.5, 2.0)
    queries = gaussian(arg_keys[3], (LAYERS, TOKENS, QH * HD), 1.0, 6.0, ((1, 64), (2, 8)))
    keys = gaussian(arg_keys[4], (LAYERS, TOKENS, KVH * HD), 1.0, 6.0, ((1, 64), (2, 8)))
    value_weight = gaussian(arg_keys[5], (LAYERS, D, KVH * HD), D ** -0.5, 0.125, ((2, 8),))
    output_weight = gaussian(arg_keys[6], (LAYERS, QH * HD, D), (QH * HD) ** -0.5, 0.125, ((1, 8), (2, 2)))
    return dict(grad_output=grad_output, layer_input=layer_input, norm_gain=norm_gain, queries=queries, keys=keys, value_weight=value_weight, output_weight=output_weight)


softcap = 50.0
query_scale = 1.0 / 12.0

def sequence_values(packed):
    query_rows, key_rows, grad_rows = packed
    query_heads = query_rows.reshape(TOK_DEV, QH, HD).astype(jnp.float32)
    key_heads = jnp.repeat(key_rows.reshape(TOK_DEV, KVH, HD), 2, axis=1).astype(jnp.float32)
    scores = jnp.einsum('qhd,khd->hqk', query_heads, key_heads)
    capped = softcap * jnp.tanh(scores * query_scale / softcap)
    positions = jnp.arange(TOK_DEV, dtype=jnp.int32)
    causal = positions[None, :] <= positions[:, None]
    weights = jnp.where(causal[None, :, :], jnp.exp(capped), 0.0)
    probs = (weights / lax.optimization_barrier(jnp.sum(weights, axis=2, keepdims=True))).astype(jnp.bfloat16)
    grad_heads = grad_rows.reshape(TOK_DEV, QH, HD).astype(jnp.float32)
    spread = jnp.einsum('hqk,qhd->khd', probs.astype(jnp.float32), grad_heads)
    summed = spread.reshape(TOK_DEV, KVH, 2, HD).sum(axis=2)
    return summed.reshape(TOK_DEV, KVH * HD).astype(jnp.bfloat16)

def reference(grad_output, layer_input, norm_gain, queries, keys, value_weight, output_weight):
    norm_scale = 1.0 / math.sqrt(TOKENS)
    sequences = TOKENS // TOK_DEV
    cotangent = grad_output
    weight_grads = [None] * LAYERS
    gain_grads = [None] * LAYERS
    group_width = KVH_DEV * HD
    for depth_index in reversed(range(LAYERS)):
        rows_full = layer_input[depth_index].astype(jnp.float32)
        inverse = lax.rsqrt(lax.optimization_barrier(jnp.mean(rows_full * rows_full, axis=1, keepdims=True)) + 1e-06)
        normed = rows_full * inverse
        gain = norm_gain[depth_index]
        scaled_input = (normed * gain).astype(jnp.bfloat16)
        context_grad = jnp.dot(cotangent, output_weight[depth_index].T, preferred_element_type=jnp.float32).astype(jnp.bfloat16)
        value_grad = lax.map(sequence_values, (queries[depth_index].reshape(sequences, TOK_DEV, QH * HD), keys[depth_index].reshape(sequences, TOK_DEV, KVH * HD), context_grad.reshape(sequences, TOK_DEV, QH * HD)))
        value_grad = value_grad.reshape(TOKENS, KVH * HD)
        weight_grads[depth_index] = jnp.dot(scaled_input.T, value_grad, preferred_element_type=jnp.float32) * norm_scale
        summed = jnp.zeros((TOKENS, D), jnp.float32)
        for shard in range(N_TENSOR):
            lower = shard * group_width
            piece = jnp.dot(value_grad[:, lower:lower + group_width], value_weight[depth_index][:, lower:lower + group_width].T, preferred_element_type=jnp.float32)
            rounded = lax.optimization_barrier(piece.astype(jnp.bfloat16))
            summed = summed + rounded.astype(jnp.float32)
        gated = summed * gain
        mixed = lax.optimization_barrier(jnp.mean(gated * normed, axis=1, keepdims=True))
        input_grad = inverse * (gated - normed * mixed)
        gain_grads[depth_index] = lax.optimization_barrier(jnp.sum(summed * normed, axis=0)) * norm_scale
        cotangent = (cotangent.astype(jnp.float32) + input_grad).astype(jnp.bfloat16)
    return (cotangent, jnp.stack(weight_grads), jnp.stack(gain_grads))
```

```python
import math

import jax
import jax.numpy as jnp
from jax import lax
from jax.experimental import pallas as pl
from jax.experimental.pallas import tpu as pltpu
from jax.sharding import PartitionSpec as P

MESH = pl.DeviceIdType.MESH
F32 = jnp.float32
BF = jnp.bfloat16

N = 8
TOK = 128
HD = 128
FB = 288
D = 2304
HALF = 1152
ROWS = 36
FAR_FIRST = (4, 3, 5, 2, 6, 1, 7)


def nt(a, b):
    return lax.dot_general(a, b, (((1,), (1,)), ((), ())), preferred_element_type=F32)


def nn(a, b):
    return lax.dot_general(a, b, (((1,), (0,)), ((), ())), preferred_element_type=F32)


def wrap(i):
    return lax.rem(i, N)


def device(y, z, g):
    return (y, z // 4, lax.rem(z, 4) * 8 + g)


def column_to_row(col):
    return jnp.transpose(jnp.broadcast_to(col, (TOK, TOK)))[0:8]


def row_to_column(row):
    return jnp.transpose(jnp.broadcast_to(row, (TOK, TOK)))


def kernel(
    cot, x, gain, q, k, vw, wo,
    out, dw_out, gain_out,
    xt, pad, gvt, probs, wot, mrx, mz, mt, vb, xn, sq, dvy, dva, mm, gx, gz, dwf, dws, dwr, cot_blk, gain_blk, inv_row, inv_col,
    sq_s, sq_r, xt_s, xt_r, sw_s, sw_r, wz_s, wz_r, wx_s, wx_r, mz_s, mz_r, mt_s, mt_r, vb_s, vb_r, xn_s, xn_r,
    dvy_s, dvy_r, dva_s, dva_r, mm_s, mm_r, gx_s, gx_r, gz_s, gz_r, dw_s, dw_r,
):
    scale = 1.0 / math.sqrt(8192.0)
    y = lax.axis_index("tensor")
    data = lax.axis_index("near") * 32 + lax.axis_index("far")
    z = data // N
    g = lax.rem(data, N)
    near = z // 4
    core = lax.rem(g, 2)
    sib = g + 1 - 2 * core

    def on_y(i):
        return device(i, z, g)

    def on_z(i):
        return device(y, i, g)

    def on_g(i):
        return device(y, z, i)

    def copy(src, dst, ss, rs, dev):
        return pltpu.make_async_remote_copy(
            src_ref=src, dst_ref=dst, send_sem=ss, recv_sem=rs, device_id=dev, device_id_type=MESH
        )

    def gather_start(buf, me, ss, rs, dev):
        for n in FAR_FIRST:
            copy(buf.at[me], buf.at[me], ss.at[n], rs.at[me], dev(wrap(me + n))).start()

    def gather_wait(buf, me, ss, rs, dev):
        for n in (1, 7, 2, 6, 3, 5, 4):
            slot = wrap(me + n)
            copy(buf.at[slot], buf.at[slot], ss.at[n], rs.at[slot], dev(slot)).wait_recv()

    def gather_sent(buf, me, ss, rs, dev):
        for n in range(1, N):
            copy(buf.at[me], buf.at[me], ss.at[n], rs.at[me], dev(wrap(me + n))).wait_send()

    def chip_start(buf, ss, rs):
        for n in (4, 2, 6):
            copy(buf.at[g], buf.at[g], ss.at[n], rs.at[g], on_g(wrap(g + n))).start()
        copy(buf.at[g], buf.at[g], ss.at[1], rs.at[g], on_g(sib)).start()

    def chip_pass(buf, ss, rs):
        for n in (2, 6, 4):
            slot = wrap(g + n)
            copy(buf.at[slot], buf.at[slot], ss.at[n], rs.at[slot], on_g(slot)).wait_recv()
            copy(buf.at[slot], buf.at[slot], ss.at[n + 1], rs.at[slot], on_g(sib)).start()

    def chip_wait(buf, ss, rs):
        for n in (0, 2, 6, 4):
            slot = wrap(sib + n)
            copy(buf.at[slot], buf.at[slot], ss.at[1], rs.at[slot], on_g(sib)).wait_recv()

    def chip_sent(buf, ss, rs):
        for n in range(1, N):
            copy(buf.at[g], buf.at[g], ss.at[n], rs.at[g], on_g(sib)).wait_send()

    barrier = pltpu.get_barrier_semaphore()

    def hello(dev):
        pl.semaphore_signal(barrier, inc=1, device_id=dev, device_id_type=MESH)

    for n in FAR_FIRST:
        hello(on_y(wrap(y + n)))
        hello(on_z(wrap(z + n)))
        hello(on_g(wrap(g + n)))
    swap_self = y == g

    @pl.when(jnp.logical_not(swap_self))
    def _():
        hello(device(g, z, y))

    plane_self = jnp.logical_and(y == z, g == y)
    for n in range(N):
        at_self = jnp.logical_and(plane_self, z == n)

        @pl.when(jnp.logical_not(at_self))
        def _():
            hello(device(z, jnp.int32(n), y))

    sq[y] = jnp.zeros((8, TOK), F32)
    pad[...] = jnp.zeros((TOK, 384), F32)
    for l in (0, 1):
        xf = x[l].astype(F32)
        sq[y, l : l + 1, :] = column_to_row(jnp.sum(xf * xf, axis=1, keepdims=True))[0:1]
    pad[:, 0:FB] = x[1].astype(F32)
    xt[y, 0:128, :] = jnp.transpose(pad[:, 0:128]).astype(BF)
    xt[y, 128:256, :] = jnp.transpose(pad[:, 128:256]).astype(BF)
    xt[y, 256:288, :] = jnp.transpose(pad[:, 256:384])[0:32].astype(BF)
    for i in range(D // 128):
        part = jnp.transpose(vw[1, 128 * i : 128 * i + 128, :].astype(F32))
        gvt[:, 128 * i : 128 * i + 128] = (part * gain[1:2, 128 * i : 128 * i + 128]).astype(BF)
    for b in range(N):

        @pl.when(y == b)
        def _():
            cot_blk[...] = cot[:, FB * b : FB * b + FB].astype(F32)
            gain_blk[...] = gain[:, FB * b : FB * b + FB]

    pl.semaphore_wait(
        barrier, 3 * (N - 1) + 1 + N - swap_self.astype(jnp.int32) - plane_self.astype(jnp.int32)
    )

    mirror = 7 - z
    rows32 = pl.multiple_of(32 * g, 32)

    def wo_chunk(l):
        return copy(
            wo.at[l, pl.ds(rows32, 32), :], wot.at[l, g], wz_s.at[l], wz_r.at[l], on_z(mirror)
        )

    def swap_slice():
        return gvt.at[
            pl.ds(pl.multiple_of(32 * lax.rem(z, 4), 32), 32), pl.ds(pl.multiple_of(HALF * near, 128), HALF)
        ]

    def swap_block():
        return vw.at[:, pl.ds(pl.multiple_of(FB * g, 16), FB), :]

    partner = device(g, z, y)
    wo_chunk(1).start()
    gather_start(sq, y, sq_s, sq_r, on_y)

    @pl.when(jnp.logical_not(swap_self))
    def _():
        copy(swap_slice(), mrx, sw_s.at[0], sw_r.at[0], partner).start()

    @pl.when(swap_self)
    def _():
        pltpu.make_async_copy(swap_slice(), mrx, sw_r.at[0]).start()

    wo_chunk(0).start()

    @pl.when(jnp.logical_not(swap_self))
    def _():
        copy(swap_block(), vb.at[y], sw_s.at[1], sw_r.at[1], partner).start()

    @pl.when(swap_self)
    def _():
        pltpu.make_async_copy(swap_block(), vb.at[y], sw_r.at[1]).start()

    gather_start(xt, y, xt_s, xt_r, on_y)

    causal = lax.broadcasted_iota(jnp.int32, (TOK, TOK), 0) <= lax.broadcasted_iota(jnp.int32, (TOK, TOK), 1)
    for l in (1, 0):
        for h in (0, 1):
            scores = nt(k[l], q[l, :, HD * h : HD * h + HD])
            weights = jnp.where(causal, jnp.exp(50.0 * jnp.tanh(scores * (1.0 / 600.0))), 0.0)
            probs[2 * l + h] = (weights / jnp.sum(weights, axis=0, keepdims=True)).astype(BF)

    mine = pl.ds(pl.multiple_of(HALF * near, 128), HALF)
    other = pl.ds(pl.multiple_of(HALF * (1 - near), 128), HALF)
    dctx1 = nt(wo[1], cot[:, mine])

    wo_chunk(1).wait_recv()
    chip_start(wot.at[1], wx_s.at[1], wx_r.at[1])

    copy(mrx, mrx, sw_s.at[0], sw_r.at[0], partner).wait_recv()
    mz[z] = nt(mrx[...], wo[0]).astype(BF)
    gather_start(mz, z, mz_s, mz_r, on_z)

    wo_chunk(0).wait_recv()
    chip_start(wot.at[0], wx_s.at[0], wx_r.at[0])

    gather_wait(sq, y, sq_s, sq_r, on_y)
    total = sq[0]
    for n in range(1, N):
        total = total + sq[n]
    inv_row[...] = lax.rsqrt(total * (1.0 / D) + 1e-6)
    for l in (0, 1):
        inv_col[l] = row_to_column(inv_row[l : l + 1, :])
        pad[:, 0:FB] = x[l].astype(F32) * inv_col[l][:, 0:1] * gain_blk[l : l + 1, :]
        xn[g, l, 0:128, :] = jnp.transpose(pad[:, 0:128]).astype(BF)
        xn[g, l, 128:256, :] = jnp.transpose(pad[:, 128:256]).astype(BF)
        xn[g, l, 256:288, :] = jnp.transpose(pad[:, 256:384])[0:32].astype(BF)

    chip_pass(wot.at[1], wx_s.at[1], wx_r.at[1])
    chip_wait(wot.at[1], wx_s.at[1], wx_r.at[1])

    def values(l, dctx):
        return nt(probs[2 * l], dctx[0:HD]) + nt(probs[2 * l + 1], dctx[HD : 2 * HD])

    dctx1 = (dctx1 + nt(wot[1].reshape(2 * HD, HALF), cot[:, other])).astype(BF)
    dvy[1, y] = values(1, dctx1).astype(BF)
    gather_start(dvy.at[1], y, dvy_s.at[1], dvy_r.at[1], on_y)
    dv1_t = nt(dctx1[0:HD], probs[2]) + nt(dctx1[HD : 2 * HD], probs[3])

    gather_wait(mz, z, mz_s, mz_r, on_z)
    m_sum = mz[0:4].reshape(HD, 2 * HD).astype(F32) + mz[4:8].reshape(HD, 2 * HD).astype(F32)
    mt[g] = jnp.transpose(m_sum).astype(BF)
    chip_start(mt, mt_s, mt_r)

    chip_pass(wot.at[0], wx_s.at[0], wx_r.at[0])
    chip_wait(wot.at[0], wx_s.at[0], wx_r.at[0])
    chip_start(xn, xn_s, xn_r)
    copy(swap_block(), vb.at[g], sw_s.at[1], sw_r.at[1], partner).wait_recv()
    chip_start(vb, vb_s, vb_r)
    wo_other = wot[0].reshape(2 * HD, HALF)
    base = nt(wo[0], cot[:, mine]) + nt(wo_other, cot[:, other])

    gather_wait(xt, y, xt_s, xt_r, on_y)
    u_t = nn(gvt[...], xt[...].reshape(D, TOK))
    part = jnp.sum(dv1_t.astype(BF).astype(F32) * u_t, axis=0, keepdims=True)
    mm[1, y] = jnp.broadcast_to(part, (8, TOK))
    gather_start(mm.at[1], y, mm_s.at[1], mm_r.at[1], on_y)
    xt_half = [xt[0:4].reshape(HALF, TOK), xt[4:8].reshape(HALF, TOK)]
    first = near == 0
    xt_mine = jnp.where(first, xt_half[0], xt_half[1])
    xt_other = jnp.where(first, xt_half[1], xt_half[0])
    y1 = nn(wo[0], xt_mine) + nn(wo_other, xt_other)

    chip_pass(mt, mt_s, mt_r)
    chip_wait(mt, mt_s, mt_r)

    def pass_heads(l):
        for n in (0, 1, 7, 2, 6, 3, 5, 4):
            head = wrap(y + n)
            if n > 0:
                copy(dvy.at[l, head], dvy.at[l, head], dvy_s.at[l, n], dvy_r.at[l, head], on_y(head)).wait_recv()

            @pl.when(head != g)
            def _():
                copy(dvy.at[l, head], dva.at[l, g], dva_s.at[l, head], dva_r.at[l, g], on_g(head)).start()

            @pl.when(head == g)
            def _():
                dva[l, g] = dvy[l, head]

    def heads_wait(l):
        for n in (1, 2, 7, 6, 3, 5, 4):
            slot = wrap(g + n)
            copy(dva.at[l, slot], dva.at[l, slot], dva_s.at[l, slot], dva_r.at[l, slot], on_g(slot)).wait_recv()

    def heads_sent(l):
        for n in range(1, N):
            slot = wrap(g + n)
            copy(dvy.at[l, slot], dva.at[l, g], dva_s.at[l, slot], dva_r.at[l, g], on_g(slot)).wait_send()

    pass_heads(1)
    corr = nt(mt[0], dvy[1, 0])
    for n in range(1, N):
        corr = corr + nt(mt[n], dvy[1, n])
    gather_wait(mm.at[1], y, mm_s.at[1], mm_r.at[1], on_y)
    total = mm[1, 0]
    for n in range(1, N):
        total = total + mm[1, n]
    inv1 = inv_row[1:2, :]
    mean1 = inv1 * total[0:1, :] * (1.0 / D)
    dctx0 = (base + inv1 * (corr - (inv1 * mean1) * y1)).astype(BF)
    dvy[0, y] = values(0, dctx0).astype(BF)
    gather_start(dvy.at[0], y, dvy_s.at[0], dvy_r.at[0], on_y)

    def scatter(l, n, start):
        at_self = jnp.logical_and(plane_self, g == n)
        away = copy(dws.at[l, n], dwr.at[l, z], dw_s.at[l, n], dw_r.at[l, z], device(g, y, jnp.int32(n)))

        @pl.when(jnp.logical_not(at_self))
        def _():
            if start:
                away.start()
            else:
                away.wait_send()

        if start:

            @pl.when(at_self)
            def _():
                pltpu.make_async_copy(dws.at[l, n], dwr.at[l, z], dw_r.at[l, z]).start()

    def weight_grad(l):
        block = nn(xn[0, l], dva[l, 0])
        for n in range(1, N):
            block = block + nn(xn[n, l], dva[l, n])
        dwf[...] = block * scale
        for n in range(N):
            dws[l, n, 0:ROWS, :] = dwf[ROWS * n : ROWS * n + ROWS, :]
            dws[l, n, ROWS:40, :] = jnp.zeros((40 - ROWS, HD), F32)
            scatter(l, n, True)

    def weight_sum(l):
        for n in range(N):
            copy(dwr.at[l, n], dwr.at[l, n], dw_s.at[l, n], dw_r.at[l, n], partner).wait_recv()
        block = dwr[l, 0]
        for n in range(1, N):
            block = block + dwr[l, n]
        dw_out[l] = block[0:ROWS]

    def input_grad(l):
        dxn = nt(dvy[l, 0], vb[0, l])
        for n in range(1, N):
            dxn = dxn + nt(dvy[l, n], vb[n, l])
        xhat = x[l].astype(F32) * inv_col[l][:, 0:1]
        gx[g, l : l + 1, 0:FB] = jnp.sum(dxn * xhat, axis=0, keepdims=True) * scale
        return xhat, dxn * gain_blk[l : l + 1, :]

    chip_pass(xn, xn_s, xn_r)
    chip_wait(xn, xn_s, xn_r)
    chip_pass(vb, vb_s, vb_r)
    chip_wait(vb, vb_s, vb_r)
    heads_wait(1)
    weight_grad(1)
    gx[g] = jnp.zeros((8, 384), F32)
    xhat, gg = input_grad(1)
    cot_blk[...] = (
        (cot_blk[...] + inv_col[1][:, 0:1] * (gg - xhat * row_to_column(mean1)[:, 0:1])).astype(BF).astype(F32)
    )

    pass_heads(0)
    xhat, gg = input_grad(0)
    mm[0, y] = column_to_row(jnp.sum(gg * xhat, axis=1, keepdims=True) * (1.0 / D))
    gather_start(mm.at[0], y, mm_s.at[0], mm_r.at[0], on_y)
    gather_start(gx, g, gx_s, gx_r, on_g)
    heads_wait(0)
    weight_grad(0)

    gather_wait(gx, g, gx_s, gx_r, on_g)
    total = gx[0]
    for n in range(1, N):
        total = total + gx[n]
    gz[z] = total
    gather_start(gz, z, gz_s, gz_r, on_z)

    gather_wait(mm.at[0], y, mm_s.at[0], mm_r.at[0], on_y)
    total = mm[0, 0]
    for n in range(1, N):
        total = total + mm[0, n]
    mean0 = row_to_column(total[0:1, :])[:, 0:1]
    out[...] = (cot_blk[...] + inv_col[0][:, 0:1] * (gg - xhat * mean0)).astype(BF)

    weight_sum(1)
    gather_wait(gz, z, gz_s, gz_r, on_z)
    total = gz[0]
    for n in range(1, N):
        total = total + gz[n]
    gain_out[...] = total[0:2, 0:FB]
    weight_sum(0)

    gather_sent(sq, y, sq_s, sq_r, on_y)
    gather_sent(xt, y, xt_s, xt_r, on_y)
    gather_sent(mz, z, mz_s, mz_r, on_z)
    gather_sent(gx, g, gx_s, gx_r, on_g)
    gather_sent(gz, z, gz_s, gz_r, on_z)
    chip_sent(mt, mt_s, mt_r)
    chip_sent(vb, vb_s, vb_r)
    chip_sent(xn, xn_s, xn_r)
    for l in (0, 1):
        wo_chunk(l).wait_send()
        chip_sent(wot.at[l], wx_s.at[l], wx_r.at[l])
        gather_sent(dvy.at[l], y, dvy_s.at[l], dvy_r.at[l], on_y)
        gather_sent(mm.at[l], y, mm_s.at[l], mm_r.at[l], on_y)
        heads_sent(l)
        for n in range(N):
            scatter(l, n, False)

    @pl.when(jnp.logical_not(swap_self))
    def _():
        copy(swap_slice(), mrx, sw_s.at[0], sw_r.at[0], partner).wait_send()
        copy(swap_block(), vb.at[y], sw_s.at[1], sw_r.at[1], partner).wait_send()


def body(grad_output, layer_input, norm_gain, queries, keys, value_weight, output_weight):
    vmem = pltpu.VMEM
    dma = pltpu.SemaphoreType.DMA
    one = [dma((N,)), dma((N,))]
    two = [dma((2, N)), dma((2, N))]
    pair = [dma((2,)), dma((2,))]
    return pl.pallas_call(
        kernel,
        out_shape=(
            jax.ShapeDtypeStruct((TOK, FB), BF),
            jax.ShapeDtypeStruct((2, ROWS, HD), F32),
            jax.ShapeDtypeStruct((2, FB), F32),
        ),
        in_specs=[pl.BlockSpec(memory_space=vmem)] * 7,
        out_specs=[pl.BlockSpec(memory_space=vmem)] * 3,
        scratch_shapes=[
            vmem((N, FB, TOK), BF),
            vmem((TOK, 384), F32),
            vmem((HD, D), BF),
            vmem((4, TOK, TOK), BF),
            vmem((2, N, 32, HALF), BF),
            vmem((32, HALF), BF),
            vmem((N, 32, 2 * HD), BF),
            vmem((N, 2 * HD, HD), BF),
            vmem((N, 2, FB, HD), BF),
            vmem((N, 2, FB, TOK), BF),
            vmem((N, 8, TOK), F32),
            vmem((2, N, TOK, HD), BF),
            vmem((2, N, TOK, HD), BF),
            vmem((2, N, 8, TOK), F32),
            vmem((N, 8, 384), F32),
            vmem((N, 8, 384), F32),
            vmem((FB, HD), F32),
            vmem((2, N, 40, HD), F32),
            vmem((2, N, 40, HD), F32),
            vmem((TOK, FB), F32),
            vmem((2, FB), F32),
            vmem((8, TOK), F32),
            vmem((2, TOK, TOK), F32),
        ]
        + one
        + one
        + pair
        + pair
        + two
        + one
        + one
        + one
        + one
        + two
        + two
        + two
        + one
        + one
        + two,
        compiler_params=pltpu.CompilerParams(
            collective_id=0, has_side_effects=True, vmem_limit_bytes=48 * 2**20
        ),
    )(grad_output, layer_input, norm_gain, queries, keys, value_weight, output_weight)


def solution(mesh):
    return jax.shard_map(
        body,
        mesh=mesh,
        in_specs=(
            P(("near", "far"), None),
            P(None, ("near", "far"), "tensor"),
            P(),
            P(None, ("near", "far"), "tensor"),
            P(None, ("near", "far"), "tensor"),
            P(None, None, "tensor"),
            P(None, "tensor", "near"),
        ),
        out_specs=(
            P(("near", "far"), "tensor"),
            P(None, ("near", "far"), "tensor"),
            P(None, "tensor"),
        ),
        check_vma=False,
    )
```

```python
import math

import jax
import jax.numpy as jnp
from jax import lax
from jax.experimental import pallas as pl
from jax.experimental.pallas import tpu as pltpu
from jax.sharding import PartitionSpec as P

MESH = pl.DeviceIdType.MESH
F32 = jnp.float32
BF = jnp.bfloat16

N = 8
TOK = 128
HD = 128
FB = 288
D = 2304
HALF = 1152
ROWS = 36
FAR_FIRST = (4, 3, 5, 2, 6, 1, 7)
NEAR_FIRST = (1, 7, 2, 6, 3, 5, 4)


def nt(a, b):
    return lax.dot_general(a, b, (((1,), (1,)), ((), ())), preferred_element_type=F32)


def nn(a, b):
    return lax.dot_general(a, b, (((1,), (0,)), ((), ())), preferred_element_type=F32)


def wrap(i):
    return lax.rem(i, N)


def device(y, z, g):
    return (y, z // 4, lax.rem(z, 4) * 8 + g)


def sum_of(ref):
    total = ref[0]
    for n in range(1, N):
        total = total + ref[n]
    return total


def kernel(
    cot_in, x_in, gain_in, q_in, k_in, vw_in, wo_in,
    out, dw_out, gain_out,
    cot, gain, q, k, vw, wo,
    xt, gcol, gvt, probs, wot, mrx, mz, mt, vb, xnb, xnf, xnp, xna, dvy, dva, mm, gys, gy, gx, gz, dwf, dws, dwr, pad, cot_blk, gain_blk, inv_row,
    in_r, xt_s, xt_r, sw_s, sw_r, wz_s, wz_r, wx_s, wx_r, mz_s, mz_r, mt_s, mt_r, vb_s, vb_r, xn_s, xn_r,
    dvy_s, dvy_r, dva_s, dva_r, mm_s, mm_r, gy_s, gy_r, gx_s, gx_r, gz_s, gz_r, dw_s, dw_r,
):
    scale = 1.0 / math.sqrt(8192.0)
    y = lax.axis_index("tensor")
    data = lax.axis_index("near") * 32 + lax.axis_index("far")
    z = data // N
    g = lax.rem(data, N)
    near = z // 4
    core = lax.rem(g, 2)
    sib = g + 1 - 2 * core

    def on_y(i):
        return device(i, z, g)

    def on_z(i):
        return device(y, i, g)

    def on_g(i):
        return device(y, z, i)

    def copy(src, dst, ss, rs, dev):
        return pltpu.make_async_remote_copy(
            src_ref=src, dst_ref=dst, send_sem=ss, recv_sem=rs, device_id=dev, device_id_type=MESH
        )

    under_way = []

    class Gather:
        def __init__(self, buf, me, sems, dev):
            self.buf, self.me, (self.ss, self.rs), self.dev = buf, me, sems, dev

        def one(self, n, slot, dev):
            return copy(self.buf.at[slot], self.buf.at[slot], self.ss.at[n], self.rs.at[slot], dev)

        def start(self):
            for n in FAR_FIRST:
                self.one(n, self.me, self.dev(wrap(self.me + n))).start()
            under_way.append(self)

        def arrived(self, n):
            slot = wrap(self.me + n)
            self.one(n, slot, self.dev(slot)).wait_recv()

        def wait(self):
            for n in NEAR_FIRST:
                self.arrived(n)
            self.wait = lambda: None

        def sent(self):
            for n in range(1, N):
                self.one(n, self.me, self.dev(wrap(self.me + n))).wait_send()

    class ChipGather(Gather):
        def start(self):
            for n in (4, 2, 6):
                self.one(n, g, on_g(wrap(g + n))).start()
            self.one(1, g, on_g(sib)).start()
            under_way.append(self)

        def wait(self):
            for n in (2, 6, 4):
                slot = wrap(g + n)
                self.one(n, slot, on_g(slot)).wait_recv()
                self.one(n + 1, slot, on_g(sib)).start()
            for n in (0, 2, 6, 4):
                slot = wrap(sib + n)
                self.one(1, slot, on_g(sib)).wait_recv()
            self.wait = lambda: None

        def sent(self):
            for n in range(1, N):
                self.one(n, g, on_g(sib)).wait_send()

    class Exchange(Gather):
        def __init__(self, src, buf, me, sems, dev):
            super().__init__(buf, me, sems, dev)
            self.src = src

        def to(self, n):
            i = wrap(self.me + n)
            return copy(self.src.at[i], self.buf.at[self.me], self.ss.at[n], self.rs.at[self.me], self.dev(i))

        def start(self):
            for n in FAR_FIRST:
                self.to(n).start()
            pltpu.make_async_copy(self.src.at[self.me], self.buf.at[self.me], self.rs.at[self.me]).start()
            under_way.append(self)

        def wait(self):
            for n in (0,) + NEAR_FIRST:
                self.arrived(n)
            self.wait = lambda: None

        def sent(self):
            for n in range(1, N):
                self.to(n).wait_send()

    class RelayGather(Gather):
        def __init__(self, src, buf, sems):
            super().__init__(buf, y, sems, on_y)
            self.src = src

        def own(self, n):
            return copy(self.src, self.buf.at[y], self.ss.at[n], self.rs.at[y], on_y(wrap(y + n)))

        def start(self):
            for n in (2, 6, 1, 7):
                self.own(n).start()
            under_way.append(self)

        def on(self, m):
            sign = 1 - 2 * lax.rem(y, 2)
            source, target = ((6, 1), (2, 7), (8 - 2 * sign, 8 + 2 * sign))[m]
            slot = wrap(y + source)
            return copy(
                self.buf.at[slot], self.buf.at[slot], self.ss.at[3 + m], self.rs.at[slot], on_y(wrap(y + target))
            )

        def relay(self):
            for n in (2, 6):
                self.arrived(n)
            for m in (2, 0, 1):
                self.on(m).start()
            self.relay = lambda: None

        def arrived(self, n):
            slot = wrap(y + n)
            self.one(0, slot, on_y(slot)).wait_recv()

        def wait(self):
            self.relay()
            for n in (1, 7, 3, 5, 4):
                self.arrived(n)
            self.wait = lambda: None

        def sent(self):
            for n in (2, 6, 1, 7):
                self.own(n).wait_send()
            for m in (0, 1, 2):
                self.on(m).wait_send()

    class Single:
        def __init__(self, src, dst, ss, rs, dev, own=None, recv=True):
            self.src, self.dst, self.rs, self.own, self.recv = src, dst, rs, own, recv
            self.away = copy(src, dst, ss, rs, dev)

        def apart(self, go):
            if self.own is None:
                go()
            else:
                pl.when(jnp.logical_not(self.own))(go)

        def start(self):
            self.apart(lambda: self.away.start())
            if self.own is not None:

                @pl.when(self.own)
                def _():
                    pltpu.make_async_copy(self.src, self.dst, self.rs).start()

            under_way.append(self)

        def wait(self):
            if self.recv:
                self.away.wait_recv()
            self.recv = False

        def sent(self):
            self.apart(lambda: self.away.wait_send())

    def drain():
        for item in under_way:
            item.wait()
        for item in under_way:
            item.sent()

    loads = {}
    for n, (name, src, dst) in enumerate(
        [
            ("vw", vw_in, vw), ("gain", gain_in, gain), ("q", q_in, q), ("k", k_in, k), ("wo", wo_in, wo), ("cot", cot_in, cot),
            ("x1", x_in.at[1], xt.at[1, y]), ("x0", x_in.at[0], xt.at[0, y]),
        ]
    ):
        loads[name] = pltpu.make_async_copy(src, dst, in_r.at[n])
        loads[name].start()

    barrier = pltpu.get_barrier_semaphore()

    def hello(dev):
        pl.semaphore_signal(barrier, inc=1, device_id=dev, device_id_type=MESH)

    for n in FAR_FIRST:
        hello(on_y(wrap(y + n)))
        hello(on_z(wrap(z + n)))
        hello(on_g(wrap(g + n)))

    shifts = tuple(c // 2 if c % 2 == 0 else (4 if c == 1 else 8 - c // 2) for c in range(N))
    shift = jnp.where(core == 0, g // 2, jnp.where(g == 1, 4, 8 - g // 2))
    head_here = shift == 0
    taker = on_y(wrap(y + 8 - shift))
    mirror = 7 - z
    rows32 = pl.multiple_of(32 * g, 32)
    mine = pl.ds(pl.multiple_of(HALF * near, 128), HALF)
    other = pl.ds(pl.multiple_of(HALF * (1 - near), 128), HALF)
    wo_chunk = [
        Single(wo_in.at[l, pl.ds(rows32, 32), :], wot.at[l, g], wz_s.at[l], wz_r.at[l], on_z(mirror)) for l in (0, 1)
    ]
    slice_rows = pl.ds(pl.multiple_of(32 * lax.rem(z, 4), 32), 32)
    swap_slice = Single(gvt.at[slice_rows, :], mrx, sw_s.at[0], sw_r.at[0], taker, head_here)
    taken = pl.ds(pl.multiple_of(FB * wrap(y + 8 - shift), 16), FB)
    swap_block = Single(vw_in.at[:, taken, :], vb.at[g], sw_s.at[1], sw_r.at[1], taker, head_here)
    inputs = [RelayGather(x_in.at[l], xt.at[l], (xt_s.at[l], xt_r.at[l])) for l in (0, 1)]
    products = Gather(mz, z, (mz_s, mz_r), on_z)
    maps = ChipGather(mt, g, (mt_s, mt_r), on_g)
    blocks = ChipGather(vb, g, (vb_s, vb_r), on_g)
    normed = [Exchange(xnp.at[l], xna.at[l], g, (xn_s.at[l], xn_r.at[l]), on_g) for l in (0, 1)]
    wo_parts = [ChipGather(wot.at[l], g, (wx_s.at[l], wx_r.at[l]), on_g) for l in (0, 1)]
    heads = [Gather(dvy.at[l], y, (dvy_s.at[l], dvy_r.at[l]), on_y) for l in (0, 1)]
    group = [Gather(dva.at[l], g, (dva_s.at[l], dva_r.at[l]), on_g) for l in (0, 1)]
    means = [Gather(mm.at[l], y, (mm_s.at[l], mm_r.at[l]), on_y) for l in (0, 1)]
    weights = [Exchange(dws.at[l], dwr.at[l], z, (dw_s.at[l], dw_r.at[l]), on_z) for l in (0, 1)]
    gains_y = Exchange(gys, gy, y, (gy_s, gy_r), on_y)
    gains_g = Gather(gx, g, (gx_s, gx_r), on_g)
    gains_z = Gather(gz, z, (gz_s, gz_r), on_z)

    pl.semaphore_wait(barrier, 3 * (N - 1))

    wo_chunk[1].start()
    inputs[1].start()

    loads["gain"].wait()
    loads["vw"].wait()
    for i in range(HALF // 128):
        rows = pl.ds(pl.multiple_of(HALF * near + 128 * i, 128), 128)
        part = jnp.transpose(vw[1, rows, :].astype(F32))
        gvt[:, 128 * i : 128 * i + 128] = (part * gain[1:2, rows]).astype(BF)
    swap_slice.start()
    wo_chunk[0].start()
    inputs[0].start()

    loads["q"].wait()
    loads["k"].wait()
    causal = lax.broadcasted_iota(jnp.int32, (TOK, TOK), 0) <= lax.broadcasted_iota(jnp.int32, (TOK, TOK), 1)
    for l in (1, 0):
        for h in (0, 1):
            scores = nt(k[l], q[l, :, HD * h : HD * h + HD])
            raised = jnp.where(causal, jnp.exp(50.0 * jnp.tanh(scores * (1.0 / 600.0))), 0.0)
            probs[2 * l + h] = (raised / jnp.sum(raised, axis=0, keepdims=True)).astype(BF)
    loads["wo"].wait()
    loads["cot"].wait()
    loads["x1"].wait()
    loads["x0"].wait()
    dctx1 = nt(wo[1], cot[:, mine])

    wo_chunk[1].wait()
    wo_parts[1].start()

    for i in range(D // 128):
        two = gain[:, 128 * i : 128 * i + 128]
        gcol[128 * i : 128 * i + 128, :] = jnp.transpose(jnp.concatenate([two, two, two, two], 0))
    swap_slice.wait()
    mz[z] = nt(mrx[...], wo[0]).astype(BF)
    products.start()
    wo_chunk[0].wait()
    wo_parts[0].start()

    inputs[1].relay()
    inputs[0].relay()

    wo_parts[1].wait()

    def values(l, dctx):
        return nt(probs[2 * l], dctx[0:HD]) + nt(probs[2 * l + 1], dctx[HD : 2 * HD])

    dctx1 = (dctx1 + nt(wot[1].reshape(2 * HD, HALF), cot[:, other])).astype(BF)
    dv = values(1, dctx1).astype(BF)
    dvy[1, y] = dv
    dva[1, g] = dv
    heads[1].start()
    group[1].start()

    def norm(l):
        total = jnp.zeros((1, TOK), F32)
        for b in range(N):
            xf = xt[l, b].astype(F32)
            total = total + jnp.sum(xf * xf, axis=0, keepdims=True)
        inv = lax.rsqrt(total * (1.0 / D) + 1e-6)
        inv_row[l : l + 1, :] = inv
        for b in range(N):
            xnb[l, b] = (xt[l, b].astype(F32) * inv * gcol[FB * b : FB * b + FB, l : l + 1]).astype(BF)

    def pack(l):
        for b in range(N):
            dwf[...] = xnb[l, b].astype(F32)
            for n in range(N):
                xnf[n, ROWS * b : ROWS * b + ROWS, :] = dwf[ROWS * n : ROWS * n + ROWS, :]
        for n in range(N):
            xnp[l, n] = xnf[n].astype(BF)
        normed[l].start()

    ones = jnp.ones((8, TOK), F32)

    def own_part(l):
        total = jnp.zeros((1, TOK), F32)
        for b in range(N):
            dxn = nt(vw[l, FB * b : FB * b + FB, :], dvy[l, y])
            prod = dxn * xnb[l, b].astype(F32)
            total = total + jnp.sum(prod, axis=0, keepdims=True)
            row = lax.dot_general(
                ones, prod, (((1,), (1,)), ((), ())), precision=lax.Precision.HIGHEST, preferred_element_type=F32
            )
            gys[b, l : l + 1, 0:FB] = row[0:1]
        mm[l, y] = jnp.broadcast_to(total * (1.0 / D), (8, TOK))
        means[l].start()

    products.wait()
    m_sum = mz[0:4].reshape(HD, 2 * HD).astype(F32) + mz[4:8].reshape(HD, 2 * HD).astype(F32)
    mt[g] = jnp.transpose(m_sum).astype(BF)
    maps.start()

    inputs[1].wait()
    gys[...] = jnp.zeros((N, 8, 384), F32)
    norm(1)
    own_part(1)
    swap_block.start()

    inputs[0].wait()
    norm(0)
    pack(0)

    wo_parts[0].wait()
    wo_other = wot[0].reshape(2 * HD, HALF)
    base = nt(wo[0], cot[:, mine]) + nt(wo_other, cot[:, other])
    xt_half = [xt[1, 0:4].reshape(HALF, TOK), xt[1, 4:8].reshape(HALF, TOK)]
    first = near == 0
    xt_mine = jnp.where(first, xt_half[0], xt_half[1])
    xt_other = jnp.where(first, xt_half[1], xt_half[0])
    y1 = nn(wo[0], xt_mine) + nn(wo_other, xt_other)
    pack(1)
    swap_block.wait()
    blocks.start()

    maps.wait()
    heads[1].wait()

    def over_heads(left, l):
        total = nt(left(0), dvy[l, wrap(y + shifts[0])])
        for n in range(1, N):
            total = total + nt(left(n), dvy[l, wrap(y + shifts[n])])
        return total

    corr = over_heads(lambda n: mt[n], 1)
    means[1].wait()
    inv1 = inv_row[1:2, :]
    mean1 = sum_of(mm.at[1])[0:1, :]
    dctx0 = (base + inv1 * (corr - (inv1 * mean1) * y1)).astype(BF)
    dv = values(0, dctx0).astype(BF)
    dvy[0, y] = dv
    dva[0, g] = dv
    group[0].start()
    heads[0].start()
    own_part(0)
    gains_y.start()

    def weight_grad(l):
        block = nn(xna[l, 0], dva[l, 0])
        for n in range(1, N):
            block = block + nn(xna[l, n], dva[l, n])
        dwf[...] = block * scale
        for n in range(N):
            dws[l, n, 0:ROWS, :] = dwf[ROWS * n : ROWS * n + ROWS, :]
            dws[l, n, ROWS:40, :] = jnp.zeros((40 - ROWS, HD), F32)
        weights[l].start()

    def weight_sum(l):
        weights[l].wait()
        dw_out[:, l, :] = sum_of(dwr.at[l])[0:ROWS]

    own_rows = pl.ds(pl.multiple_of(FB * y, 32), FB)

    def input_grad(l, mean):
        dxn = over_heads(lambda n: vb[n, l], l)
        inv = inv_row[l : l + 1, :]
        return inv * (dxn * gcol[own_rows, l : l + 1] - xt[l, y].astype(F32) * (inv * mean))

    normed[1].wait()
    group[1].wait()
    weight_grad(1)
    normed[0].wait()
    group[0].wait()
    weight_grad(0)

    gains_y.wait()
    gx[g] = sum_of(gy)
    gains_g.start()

    for b in range(N):

        @pl.when(y == b)
        def _():
            pad[:, 0:FB] = cot[:, FB * b : FB * b + FB].astype(F32)
            gain_blk[...] = gain[:, FB * b : FB * b + FB]

    cot_blk[0:128, :] = jnp.transpose(pad[:, 0:128])
    cot_blk[128:256, :] = jnp.transpose(pad[:, 128:256])
    cot_blk[256:288, :] = jnp.transpose(pad[:, 256:384])[0:32]
    blocks.wait()
    cot1 = (cot_blk[...] + input_grad(1, mean1)).astype(BF).astype(F32)

    gains_g.wait()
    gz[z] = sum_of(gx)
    gains_z.start()

    heads[0].wait()
    means[0].wait()
    out[...] = (cot1 + input_grad(0, sum_of(mm.at[0])[0:1, :])).astype(BF)

    weight_sum(1)
    weight_sum(0)
    gains_z.wait()
    gain_out[...] = sum_of(gz)[0:2, 0:FB] * scale / gain_blk[...]
    drain()


def body(grad_output, layer_input, norm_gain, queries, keys, value_weight, output_weight):
    vmem = pltpu.VMEM
    dma = pltpu.SemaphoreType.DMA
    one = [dma((N,)), dma((N,))]
    two = [dma((2, N)), dma((2, N))]
    pair = [dma((2,)), dma((2,))]
    hbm = pl.BlockSpec(memory_space=pltpu.HBM)
    out, weights, gains = pl.pallas_call(
        kernel,
        out_shape=(
            jax.ShapeDtypeStruct((FB, TOK), BF),
            jax.ShapeDtypeStruct((ROWS, 2, HD), F32),
            jax.ShapeDtypeStruct((2, FB), F32),
        ),
        in_specs=[hbm] * 7,
        out_specs=[pl.BlockSpec(memory_space=vmem)] * 3,
        scratch_shapes=[
            vmem((TOK, D), BF),
            vmem((2, D), F32),
            vmem((2, TOK, 2 * HD), BF),
            vmem((2, TOK, HD), BF),
            vmem((2, D, HD), BF),
            vmem((2, 2 * HD, HALF), BF),
            vmem((2, N, FB, TOK), BF),
            vmem((D, 8), F32),
            vmem((HD, HALF), BF),
            vmem((4, TOK, TOK), BF),
            vmem((2, N, 32, HALF), BF),
            vmem((32, HALF), BF),
            vmem((N, 32, 2 * HD), BF),
            vmem((N, 2 * HD, HD), BF),
            vmem((N, 2, FB, HD), BF),
            vmem((2, N, FB, TOK), BF),
            vmem((N, FB, TOK), F32),
            vmem((2, N, FB, TOK), BF),
            vmem((2, N, FB, TOK), BF),
            vmem((2, N, TOK, HD), BF),
            vmem((2, N, TOK, HD), BF),
            vmem((2, N, 8, TOK), F32),
            vmem((N, 8, 384), F32),
            vmem((N, 8, 384), F32),
            vmem((N, 8, 384), F32),
            vmem((N, 8, 384), F32),
            vmem((FB, HD), F32),
            vmem((2, N, 40, HD), F32),
            vmem((2, N, 40, HD), F32),
            vmem((TOK, 384), F32),
            vmem((FB, TOK), F32),
            vmem((2, FB), F32),
            vmem((8, TOK), F32),
        ]
        + [dma((8,))]
        + two
        + pair
        + pair
        + two
        + one
        + one
        + one
        + two
        + two
        + two
        + two
        + one
        + one
        + one
        + two,
        compiler_params=pltpu.CompilerParams(
            collective_id=0, has_side_effects=True, vmem_limit_bytes=63 * 2**20
        ),
    )(grad_output, jnp.swapaxes(layer_input, 1, 2), norm_gain, queries, keys, value_weight, output_weight)
    return jnp.swapaxes(out, 0, 1), jnp.swapaxes(weights, 0, 1), gains


def solution(mesh):
    return jax.shard_map(
        body,
        mesh=mesh,
        in_specs=(
            P(("near", "far"), None),
            P(None, ("near", "far"), "tensor"),
            P(),
            P(None, ("near", "far"), "tensor"),
            P(None, ("near", "far"), "tensor"),
            P(None, None, "tensor"),
            P(None, "tensor", "near"),
        ),
        out_specs=(
            P(("near", "far"), "tensor"),
            P(None, ("near", "far"), "tensor"),
            P(None, "tensor"),
        ),
        check_vma=False,
    )
```

```python
import math

import jax
import jax.numpy as jnp
from jax import lax
from jax.experimental import pallas as pl
from jax.experimental.pallas import tpu as pltpu
from jax.sharding import PartitionSpec as P

MESH = pl.DeviceIdType.MESH
F32 = jnp.float32
BF = jnp.bfloat16

N = 8
TOK = 128
HD = 128
FB = 288
D = 2304
HALF = 1152
ROWS = 36
FAR_FIRST = (4, 3, 5, 2, 6, 1, 7)
NEAR_FIRST = (1, 7, 2, 6, 3, 5, 4)


def nt(a, b):
    return lax.dot_general(a, b, (((1,), (1,)), ((), ())), preferred_element_type=F32)


def nn(a, b):
    return lax.dot_general(a, b, (((1,), (0,)), ((), ())), preferred_element_type=F32)


def wrap(i):
    return lax.rem(i, N)


def device(y, z, g):
    return (y, z // 4, lax.rem(z, 4) * 8 + g)


def sum_of(ref):
    total = ref[0]
    for n in range(1, N):
        total = total + ref[n]
    return total


def kernel(
    cot_in, x_in, gain_in, q_in, k_in, vw_in, wo_in,
    out, dw_out, gain_out,
    cot, gain, q, k, vw, wo, x0,
    xt, x0p, x0a, x0y, x0w, gcol, gvt, probs, wot, mrx, mz, mt, vb, xnb, xnf, xnp, xna, dvy, dva, sq, mm, gx, gz, dwf, dws, dwr, pad, cot_blk,
    in_r, xt_s, xt_r, x0a_s, x0a_r, x0y_s, x0y_r, sw_s, sw_r, wz_s, wz_r, wx_s, wx_r, mz_s, mz_r, mt_s, mt_r, vb_s, vb_r, xn_s, xn_r,
    dvy_s, dvy_r, dva_s, dva_r, sq_s, sq_r, mm_s, mm_r, gx_s, gx_r, gz_s, gz_r, dw_s, dw_r,
):
    scale = 1.0 / math.sqrt(8192.0)
    y = lax.axis_index("tensor")
    data = lax.axis_index("near") * 32 + lax.axis_index("far")
    z = data // N
    g = lax.rem(data, N)
    near = z // 4
    core = lax.rem(g, 2)
    sib = g + 1 - 2 * core

    def on_y(i):
        return device(i, z, g)

    def on_z(i):
        return device(y, i, g)

    def on_g(i):
        return device(y, z, i)

    def copy(src, dst, ss, rs, dev):
        return pltpu.make_async_remote_copy(
            src_ref=src, dst_ref=dst, send_sem=ss, recv_sem=rs, device_id=dev, device_id_type=MESH
        )

    under_way = []

    class Gather:
        def __init__(self, buf, me, sems, dev):
            self.buf, self.me, (self.ss, self.rs), self.dev = buf, me, sems, dev

        def one(self, n, slot, dev):
            return copy(self.buf.at[slot], self.buf.at[slot], self.ss.at[n], self.rs.at[slot], dev)

        def start(self):
            for n in FAR_FIRST:
                self.one(n, self.me, self.dev(wrap(self.me + n))).start()
            under_way.append(self)

        def arrived(self, n):
            slot = wrap(self.me + n)
            self.one(n, slot, self.dev(slot)).wait_recv()

        def wait(self):
            for n in NEAR_FIRST:
                self.arrived(n)
            self.wait = lambda: None

        def sent(self):
            for n in range(1, N):
                self.one(n, self.me, self.dev(wrap(self.me + n))).wait_send()

    class ChipGather(Gather):
        def start(self):
            for n in (4, 2, 6):
                self.one(n, g, on_g(wrap(g + n))).start()
            self.one(1, g, on_g(sib)).start()
            under_way.append(self)

        def pass_on(self):
            for n in (2, 6, 4):
                slot = wrap(g + n)
                self.one(n, slot, on_g(slot)).wait_recv()
                self.one(n + 1, slot, on_g(sib)).start()
            self.pass_on = lambda: None

        def wait(self):
            self.pass_on()
            for n in (0, 2, 6, 4):
                slot = wrap(sib + n)
                self.one(1, slot, on_g(sib)).wait_recv()
            self.wait = lambda: None

        def sent(self):
            for n in range(1, N):
                self.one(n, g, on_g(sib)).wait_send()

    class Exchange(Gather):
        def __init__(self, src, buf, me, sems, dev):
            super().__init__(buf, me, sems, dev)
            self.src = src

        def to(self, n):
            i = wrap(self.me + n)
            return copy(self.src.at[i], self.buf.at[self.me], self.ss.at[n], self.rs.at[self.me], self.dev(i))

        def start(self):
            for n in FAR_FIRST:
                self.to(n).start()
            pltpu.make_async_copy(self.src.at[self.me], self.buf.at[self.me], self.rs.at[self.me]).start()
            under_way.append(self)

        def wait(self):
            for n in (0,) + NEAR_FIRST:
                self.arrived(n)
            self.wait = lambda: None

        def sent(self):
            for n in range(1, N):
                self.to(n).wait_send()

    class RelayGather(Gather):
        def __init__(self, src, buf, sems):
            super().__init__(buf, y, sems, on_y)
            self.src = src

        def own(self, n):
            return copy(self.src, self.buf.at[y], self.ss.at[n], self.rs.at[y], on_y(wrap(y + n)))

        def start(self):
            for n in (2, 6, 1, 7):
                self.own(n).start()
            under_way.append(self)

        def on(self, m):
            sign = 1 - 2 * lax.rem(y, 2)
            source, target = ((6, 1), (2, 7), (8 - 2 * sign, 8 + 2 * sign))[m]
            slot = wrap(y + source)
            return copy(
                self.buf.at[slot], self.buf.at[slot], self.ss.at[3 + m], self.rs.at[slot], on_y(wrap(y + target))
            )

        def relay(self):
            for n in (2, 6):
                self.arrived(n)
            for m in (2, 0, 1):
                self.on(m).start()
            self.relay = lambda: None

        def arrived(self, n):
            slot = wrap(y + n)
            self.one(0, slot, on_y(slot)).wait_recv()

        def wait(self):
            self.relay()
            for n in (1, 7, 3, 5, 4):
                self.arrived(n)
            self.wait = lambda: None

        def sent(self):
            for n in (2, 6, 1, 7):
                self.own(n).wait_send()
            for m in (0, 1, 2):
                self.on(m).wait_send()

    class Single:
        def __init__(self, src, dst, ss, rs, dev, own=None, recv=True):
            self.src, self.dst, self.rs, self.own, self.recv = src, dst, rs, own, recv
            self.away = copy(src, dst, ss, rs, dev)

        def apart(self, go):
            if self.own is None:
                go()
            else:
                pl.when(jnp.logical_not(self.own))(go)

        def start(self):
            self.apart(lambda: self.away.start())
            if self.own is not None:

                @pl.when(self.own)
                def _():
                    pltpu.make_async_copy(self.src, self.dst, self.rs).start()

            under_way.append(self)

        def wait(self):
            if self.recv:
                self.away.wait_recv()
            self.recv = False

        def sent(self):
            self.apart(lambda: self.away.wait_send())

    def drain():
        for item in under_way:
            item.wait()
        for item in under_way:
            item.sent()

    loads = {}
    for n, (name, src, dst) in enumerate(
        [
            ("x0", x_in.at[0], x0), ("gain", gain_in, gain), ("vw", vw_in, vw), ("q", q_in, q), ("k", k_in, k),
            ("wo", wo_in, wo), ("cot", cot_in, cot), ("x1", x_in.at[1], xt.at[y]),
        ]
    ):
        loads[name] = pltpu.make_async_copy(src, dst, in_r.at[n])
        loads[name].start()

    barrier = pltpu.get_barrier_semaphore()

    def hello(dev):
        pl.semaphore_signal(barrier, inc=1, device_id=dev, device_id_type=MESH)

    for n in FAR_FIRST:
        hello(on_y(wrap(y + n)))
        hello(on_z(wrap(z + n)))
        hello(on_g(wrap(g + n)))

    shifts = tuple(c // 2 if c % 2 == 0 else (4 if c == 1 else 8 - c // 2) for c in range(N))
    shift = jnp.where(core == 0, g // 2, jnp.where(g == 1, 4, 8 - g // 2))
    head_here = shift == 0
    taker = on_y(wrap(y + 8 - shift))
    mirror = 7 - z
    rows32 = pl.multiple_of(32 * g, 32)
    mine = pl.ds(pl.multiple_of(HALF * near, 128), HALF)
    other = pl.ds(pl.multiple_of(HALF * (1 - near), 128), HALF)
    wo_chunk = [
        Single(wo_in.at[l, pl.ds(rows32, 32), :], wot.at[l, g], wz_s.at[l], wz_r.at[l], on_z(mirror)) for l in (0, 1)
    ]
    slice_rows = pl.ds(pl.multiple_of(32 * lax.rem(z, 4), 32), 32)
    swap_slice = Single(gvt.at[slice_rows, :], mrx, sw_s.at[0], sw_r.at[0], taker, head_here)
    taken = pl.ds(pl.multiple_of(FB * wrap(y + 8 - shift), 16), FB)
    swap_block = Single(vw_in.at[:, taken, :], vb.at[g], sw_s.at[1], sw_r.at[1], taker, head_here)
    inputs = RelayGather(x_in.at[1], xt, (xt_s, xt_r))
    squares = Gather(sq, y, (sq_s, sq_r), on_y)
    mixed = Exchange(x0p, x0a, g, (x0a_s, x0a_r), on_g)
    mixed_y = RelayGather(x0y.at[y], x0y, (x0y_s, x0y_r))
    products = Gather(mz, z, (mz_s, mz_r), on_z)
    maps = ChipGather(mt, g, (mt_s, mt_r), on_g)
    blocks = ChipGather(vb, g, (vb_s, vb_r), on_g)
    normed = Exchange(xnp, xna, g, (xn_s, xn_r), on_g)
    wo_parts = [ChipGather(wot.at[l], g, (wx_s.at[l], wx_r.at[l]), on_g) for l in (0, 1)]
    heads = [Gather(dvy.at[l], y, (dvy_s.at[l], dvy_r.at[l]), on_y) for l in (0, 1)]
    group = [Gather(dva.at[l], g, (dva_s.at[l], dva_r.at[l]), on_g) for l in (0, 1)]
    means = [Gather(mm.at[l], y, (mm_s.at[l], mm_r.at[l]), on_y) for l in (0, 1)]
    weights = [Exchange(dws.at[l], dwr.at[l], z, (dw_s.at[l], dw_r.at[l]), on_z) for l in (0, 1)]
    gains_g = Gather(gx, g, (gx_s, gx_r), on_g)
    gains_z = Gather(gz, z, (gz_s, gz_r), on_z)

    pl.semaphore_wait(barrier, 3 * (N - 1))

    wo_chunk[1].start()
    inputs.start()
    loads["x0"].wait()
    xf = x0[...].astype(F32)
    sq[y] = jnp.broadcast_to(jnp.sum(xf * xf, axis=0, keepdims=True), (8, TOK))
    squares.start()

    loads["gain"].wait()
    loads["vw"].wait()
    for i in range(HALF // 128):
        rows = pl.ds(pl.multiple_of(HALF * near + 128 * i, 128), 128)
        part = jnp.transpose(vw[1, rows, :].astype(F32))
        gvt[:, 128 * i : 128 * i + 128] = (part * gain[1:2, rows]).astype(BF)
    swap_slice.start()
    wo_chunk[0].start()
    swap_block.start()

    loads["q"].wait()
    loads["k"].wait()
    causal = lax.broadcasted_iota(jnp.int32, (TOK, TOK), 0) <= lax.broadcasted_iota(jnp.int32, (TOK, TOK), 1)

    def attend(l):
        for h in (0, 1):
            scores = nt(k[l], q[l, :, HD * h : HD * h + HD])
            raised = jnp.where(causal, jnp.exp(50.0 * jnp.tanh(scores * (1.0 / 600.0))), 0.0)
            probs[2 * l + h] = (raised / jnp.sum(raised, axis=0, keepdims=True)).astype(BF)

    attend(1)
    loads["wo"].wait()
    loads["cot"].wait()
    loads["x1"].wait()
    dctx1 = nt(wo[1], cot[:, mine])

    wo_chunk[1].wait()
    wo_parts[1].start()
    swap_slice.wait()
    mz[z] = nt(mrx[...], wo[0]).astype(BF)
    products.start()

    for i in range(D // 128):
        two = gain[:, 128 * i : 128 * i + 128]
        gcol[128 * i : 128 * i + 128, :] = jnp.transpose(jnp.concatenate([two, two, two, two], 0))
    own_rows = pl.ds(pl.multiple_of(FB * y, 32), FB)

    squares.wait()
    inv0 = lax.rsqrt(sum_of(sq)[0:1] * (1.0 / D) + 1e-6)
    dwf[...] = x0[...].astype(F32) * inv0 * gcol[own_rows, 0:1]
    for n in range(N):
        x0p[n] = jnp.concatenate([dwf[ROWS * n : ROWS * n + ROWS, :], jnp.zeros((48 - ROWS, TOK), F32)], 0).astype(BF)
    mixed.start()

    wo_chunk[0].wait()
    wo_parts[0].start()

    inputs.relay()
    wo_parts[1].wait()

    def values(l, dctx):
        return nt(probs[2 * l], dctx[0:HD]) + nt(probs[2 * l + 1], dctx[HD : 2 * HD])

    dctx1 = (dctx1 + nt(wot[1].reshape(2 * HD, HALF), cot[:, other])).astype(BF)
    dv = values(1, dctx1).astype(BF)
    dvy[1, y] = dv
    dva[1, g] = dv
    heads[1].start()
    group[1].start()
    attend(0)

    def regroup(part):
        for b in range(N):
            dwf[...] = part(b).astype(F32)
            for n in range(N):
                xnf[n, ROWS * b : ROWS * b + ROWS, :] = dwf[ROWS * n : ROWS * n + ROWS, :]

    products.wait()
    m_sum = mz[0:4].reshape(HD, 2 * HD).astype(F32) + mz[4:8].reshape(HD, 2 * HD).astype(F32)
    mt[g] = jnp.transpose(m_sum).astype(BF)
    maps.start()

    mixed.wait()
    for n in range(N):
        dwf[ROWS * n : ROWS * n + ROWS, :] = x0a[n].astype(F32)[0:ROWS]
    x0y[y] = dwf[...].astype(BF)
    mixed_y.start()

    swap_block.wait()
    blocks.start()
    wo_parts[0].pass_on()

    inputs.wait()
    total = jnp.zeros((1, TOK), F32)
    for b in range(N):
        xf = xt[b].astype(F32)
        total = total + jnp.sum(xf * xf, axis=0, keepdims=True)
    inv1 = lax.rsqrt(total * (1.0 / D) + 1e-6)
    total = jnp.zeros((1, TOK), F32)
    for b in range(N):
        xnb[b] = (xt[b].astype(F32) * inv1 * gcol[FB * b : FB * b + FB, 1:2]).astype(BF)
        dxn = nt(vw[1, FB * b : FB * b + FB, :], dvy[1, y])
        total = total + jnp.sum(dxn * xnb[b].astype(F32), axis=0, keepdims=True)
    mm[1, y] = jnp.broadcast_to(total * (1.0 / D), (8, TOK))
    means[1].start()

    maps.pass_on()
    wo_parts[0].wait()
    wo_other = wot[0].reshape(2 * HD, HALF)
    base = nt(wo[0], cot[:, mine]) + nt(wo_other, cot[:, other])
    xt_half = [xt[0:4].reshape(HALF, TOK), xt[4:8].reshape(HALF, TOK)]
    first = near == 0
    xt_mine = jnp.where(first, xt_half[0], xt_half[1])
    xt_other = jnp.where(first, xt_half[1], xt_half[0])
    y1 = nn(wo[0], xt_mine) + nn(wo_other, xt_other)
    regroup(lambda b: xnb[b])
    for n in range(N):
        xnp[n] = xnf[n].astype(BF)
    normed.start()
    mixed_y.relay()

    maps.wait()
    heads[1].wait()

    def over_heads(left, l):
        total = nt(left(0), dvy[l, wrap(y + shifts[0])])
        for n in range(1, N):
            total = total + nt(left(n), dvy[l, wrap(y + shifts[n])])
        return total

    corr = over_heads(lambda n: mt[n], 1)
    means[1].wait()
    mean1 = sum_of(mm.at[1])[0:1, :]
    dctx0 = (base + inv1 * (corr - (inv1 * mean1) * y1)).astype(BF)
    dv = values(0, dctx0).astype(BF)
    dvy[0, y] = dv
    dva[0, g] = dv
    group[0].start()
    heads[0].start()
    blocks.pass_on()

    for b in range(N):

        @pl.when(y == b)
        def _():
            pad[:, 0:FB] = cot[:, FB * b : FB * b + FB].astype(F32)

    cot_blk[0:128, :] = jnp.transpose(pad[:, 0:128])
    cot_blk[128:256, :] = jnp.transpose(pad[:, 128:256])
    cot_blk[256:288, :] = jnp.transpose(pad[:, 256:384])[0:32]

    def weight_grad(l, left):
        block = nn(left(0), dva[l, 0])
        for n in range(1, N):
            block = block + nn(left(n), dva[l, n])
        dwf[...] = block * scale
        for n in range(N):
            dws[l, n, 0:ROWS, :] = dwf[ROWS * n : ROWS * n + ROWS, :]
            dws[l, n, ROWS:40, :] = jnp.zeros((40 - ROWS, HD), F32)
        weights[l].start()

    def weight_sum(l):
        weights[l].wait()
        dw_out[:, l, :] = sum_of(dwr.at[l])[0:ROWS]

    ones = jnp.ones((8, TOK), F32)

    def input_grad(l, own, inv):
        dxn = over_heads(lambda n: vb[n, l], l)
        xhat = own * inv
        row = lax.dot_general(
            ones, dxn * xhat, (((1,), (1,)), ((), ())), precision=lax.Precision.HIGHEST, preferred_element_type=F32
        )
        gx[g, l : l + 1, 0:FB] = row[0:1] * scale
        return xhat, dxn * gcol[own_rows, l : l + 1]

    normed.wait()
    group[1].wait()
    weight_grad(1, lambda n: xna[n])
    mixed_y.wait()
    regroup(lambda b: x0y[b])
    for n in range(N):
        x0w[n] = xnf[n].astype(BF)
    gx[g] = jnp.zeros((8, 384), F32)
    blocks.wait()
    xhat, gg = input_grad(1, xt[y].astype(F32), inv1)
    cot_blk[...] = (cot_blk[...] + inv1 * (gg - xhat * mean1)).astype(BF).astype(F32)

    group[0].wait()
    weight_grad(0, lambda n: x0w[n])

    heads[0].wait()
    xhat, gg = input_grad(0, x0[...].astype(F32), inv0)
    gains_g.start()
    mm[0, y] = jnp.broadcast_to(jnp.sum(gg * xhat, axis=0, keepdims=True) * (1.0 / D), (8, TOK))
    means[0].start()
    gains_g.wait()
    gz[z] = sum_of(gx)
    gains_z.start()

    means[0].wait()
    out[...] = (cot_blk[...] + inv0 * (gg - xhat * sum_of(mm.at[0])[0:1, :])).astype(BF)

    weight_sum(1)
    weight_sum(0)
    gains_z.wait()
    gain_out[...] = sum_of(gz)[0:2, 0:FB]
    drain()


def body(grad_output, layer_input, norm_gain, queries, keys, value_weight, output_weight):
    vmem = pltpu.VMEM
    dma = pltpu.SemaphoreType.DMA
    one = [dma((N,)), dma((N,))]
    two = [dma((2, N)), dma((2, N))]
    pair = [dma((2,)), dma((2,))]
    hbm = pl.BlockSpec(memory_space=pltpu.HBM)
    out, weights, gains = pl.pallas_call(
        kernel,
        out_shape=(
            jax.ShapeDtypeStruct((FB, TOK), BF),
            jax.ShapeDtypeStruct((ROWS, 2, HD), F32),
            jax.ShapeDtypeStruct((2, FB), F32),
        ),
        in_specs=[hbm] * 7,
        out_specs=[pl.BlockSpec(memory_space=vmem)] * 3,
        scratch_shapes=[
            vmem((TOK, D), BF),
            vmem((2, D), F32),
            vmem((2, TOK, 2 * HD), BF),
            vmem((2, TOK, HD), BF),
            vmem((2, D, HD), BF),
            vmem((2, 2 * HD, HALF), BF),
            vmem((FB, TOK), BF),
            vmem((N, FB, TOK), BF),
            vmem((N, 48, TOK), BF),
            vmem((N, 48, TOK), BF),
            vmem((N, FB, TOK), BF),
            vmem((N, FB, TOK), BF),
            vmem((D, 8), F32),
            vmem((HD, HALF), BF),
            vmem((4, TOK, TOK), BF),
            vmem((2, N, 32, HALF), BF),
            vmem((32, HALF), BF),
            vmem((N, 32, 2 * HD), BF),
            vmem((N, 2 * HD, HD), BF),
            vmem((N, 2, FB, HD), BF),
            vmem((N, FB, TOK), BF),
            vmem((N, FB, TOK), F32),
            vmem((N, FB, TOK), BF),
            vmem((N, FB, TOK), BF),
            vmem((2, N, TOK, HD), BF),
            vmem((2, N, TOK, HD), BF),
            vmem((N, 8, TOK), F32),
            vmem((2, N, 8, TOK), F32),
            vmem((N, 8, 384), F32),
            vmem((N, 8, 384), F32),
            vmem((FB, HD), F32),
            vmem((2, N, 40, HD), F32),
            vmem((2, N, 40, HD), F32),
            vmem((TOK, 384), F32),
            vmem((FB, TOK), F32),
        ]
        + [dma((8,))]
        + one
        + one
        + one
        + pair
        + pair
        + two
        + one
        + one
        + one
        + one
        + two
        + two
        + one
        + two
        + one
        + one
        + two,
        compiler_params=pltpu.CompilerParams(
            collective_id=0, has_side_effects=True, vmem_limit_bytes=63 * 2**20
        ),
    )(grad_output, jnp.swapaxes(layer_input, 1, 2), norm_gain, queries, keys, value_weight, output_weight)
    return jnp.swapaxes(out, 0, 1), jnp.swapaxes(weights, 0, 1), gains


def solution(mesh):
    return jax.shard_map(
        body,
        mesh=mesh,
        in_specs=(
            P(("near", "far"), None),
            P(None, ("near", "far"), "tensor"),
            P(),
            P(None, ("near", "far"), "tensor"),
            P(None, ("near", "far"), "tensor"),
            P(None, None, "tensor"),
            P(None, "tensor", "near"),
        ),
        out_specs=(
            P(("near", "far"), "tensor"),
            P(None, ("near", "far"), "tensor"),
            P(None, "tensor"),
        ),
        check_vma=False,
    )
```

```python
import math

import jax
import jax.numpy as jnp
from jax import lax
from jax.experimental import pallas as pl
from jax.experimental.pallas import tpu as pltpu
from jax.sharding import PartitionSpec as P

MESH = pl.DeviceIdType.MESH
F32 = jnp.float32
BF = jnp.bfloat16

N = 8
TOK = 128
HD = 128
FB = 288
D = 2304
HALF = 1152
ROWS = 36
FAR_FIRST = (4, 3, 5, 2, 6, 1, 7)
NEAR_FIRST = (1, 7, 2, 6, 3, 5, 4)


def nt(a, b):
    return lax.dot_general(a, b, (((1,), (1,)), ((), ())), preferred_element_type=F32)


def nn(a, b):
    return lax.dot_general(a, b, (((1,), (0,)), ((), ())), preferred_element_type=F32)


def wrap(i):
    return lax.rem(i, N)


def device(y, z, g):
    return (y, z // 4, lax.rem(z, 4) * 8 + g)


def sum_of(ref):
    total = ref[0]
    for n in range(1, N):
        total = total + ref[n]
    return total


def kernel(
    cot_in, x_in, gain_in, q_in, k_in, vw_in, wo_in,
    out, dw_out, gain_out,
    cot, gain, q, k, vw, wo, x0,
    xt, x0p, x0a, x0y, x0w, gcol, gvt, probs, wot, mrx, mz, mt, vb, xnb, xnf, xna, dvy, dva, sq, mm, gx, gz, dwf, dws, dwr, pad, cot_blk,
    in_r, xt_s, xt_r, x0a_s, x0a_r, x0y_s, x0y_r, sw_s, sw_r, wz_s, wz_r, wx_s, wx_r, mz_s, mz_r, mt_s, mt_r, vb_s, vb_r, xn_s, xn_r,
    dvy_s, dvy_r, dva_s, dva_r, sq_s, sq_r, mm_s, mm_r, gx_s, gx_r, gz_s, gz_r, dw_s, dw_r,
):
    scale = 1.0 / math.sqrt(8192.0)
    y = lax.axis_index("tensor")
    data = lax.axis_index("near") * 32 + lax.axis_index("far")
    z = data // N
    g = lax.rem(data, N)
    near = z // 4
    core = lax.rem(g, 2)
    sib = g + 1 - 2 * core

    def on_y(i):
        return device(i, z, g)

    def on_z(i):
        return device(y, i, g)

    def on_g(i):
        return device(y, z, i)

    def copy(src, dst, ss, rs, dev):
        return pltpu.make_async_remote_copy(
            src_ref=src, dst_ref=dst, send_sem=ss, recv_sem=rs, device_id=dev, device_id_type=MESH
        )

    under_way = []

    class Gather:
        def __init__(self, buf, me, sems, dev):
            self.buf, self.me, (self.ss, self.rs), self.dev = buf, me, sems, dev

        def one(self, n, slot, dev):
            return copy(self.buf.at[slot], self.buf.at[slot], self.ss.at[n], self.rs.at[slot], dev)

        def start(self):
            for n in FAR_FIRST:
                self.one(n, self.me, self.dev(wrap(self.me + n))).start()
            under_way.append(self)

        def arrived(self, n):
            slot = wrap(self.me + n)
            self.one(n, slot, self.dev(slot)).wait_recv()

        def wait(self):
            for n in NEAR_FIRST:
                self.arrived(n)
            self.wait = lambda: None

        def sent(self):
            for n in range(1, N):
                self.one(n, self.me, self.dev(wrap(self.me + n))).wait_send()

    class ChipGather(Gather):
        def start(self):
            for n in (4, 2, 6):
                self.one(n, g, on_g(wrap(g + n))).start()
            self.one(1, g, on_g(sib)).start()
            under_way.append(self)

        def pass_on(self):
            for n in (2, 6, 4):
                slot = wrap(g + n)
                self.one(n, slot, on_g(slot)).wait_recv()
                self.one(n + 1, slot, on_g(sib)).start()
            self.pass_on = lambda: None

        def wait(self):
            self.pass_on()
            for n in (0, 2, 6, 4):
                slot = wrap(sib + n)
                self.one(1, slot, on_g(sib)).wait_recv()
            self.wait = lambda: None

        def sent(self):
            for n in range(1, N):
                self.one(n, g, on_g(sib)).wait_send()

    class Exchange(Gather):
        def __init__(self, src, buf, me, sems, dev):
            super().__init__(buf, me, sems, dev)
            self.src = src

        def to(self, n):
            i = wrap(self.me + n)
            return copy(self.src.at[i], self.buf.at[self.me], self.ss.at[n], self.rs.at[self.me], self.dev(i))

        def start(self):
            for n in FAR_FIRST:
                self.to(n).start()
            pltpu.make_async_copy(self.src.at[self.me], self.buf.at[self.me], self.rs.at[self.me]).start()
            under_way.append(self)

        def wait(self):
            for n in (0,) + NEAR_FIRST:
                self.arrived(n)
            self.wait = lambda: None

        def sent(self):
            for n in range(1, N):
                self.to(n).wait_send()

    class RelayGather(Gather):
        def __init__(self, src, buf, sems):
            super().__init__(buf, y, sems, on_y)
            self.src = src

        def own(self, n):
            return copy(self.src, self.buf.at[y], self.ss.at[n], self.rs.at[y], on_y(wrap(y + n)))

        def start(self):
            for n in (2, 6, 1, 7):
                self.own(n).start()
            under_way.append(self)

        def on(self, m):
            sign = 1 - 2 * lax.rem(y, 2)
            source, target = ((6, 1), (2, 7), (8 - 2 * sign, 8 + 2 * sign))[m]
            slot = wrap(y + source)
            return copy(
                self.buf.at[slot], self.buf.at[slot], self.ss.at[3 + m], self.rs.at[slot], on_y(wrap(y + target))
            )

        def relay(self):
            for n in (2, 6):
                self.arrived(n)
            for m in (2, 0, 1):
                self.on(m).start()
            self.relay = lambda: None

        def arrived(self, n):
            slot = wrap(y + n)
            self.one(0, slot, on_y(slot)).wait_recv()

        def wait(self):
            self.relay()
            for n in (1, 7, 3, 5, 4):
                self.arrived(n)
            self.wait = lambda: None

        def sent(self):
            for n in (2, 6, 1, 7):
                self.own(n).wait_send()
            for m in (0, 1, 2):
                self.on(m).wait_send()

    class Single:
        def __init__(self, src, dst, ss, rs, dev, own=None, recv=True):
            self.src, self.dst, self.rs, self.own, self.recv = src, dst, rs, own, recv
            self.away = copy(src, dst, ss, rs, dev)

        def apart(self, go):
            if self.own is None:
                go()
            else:
                pl.when(jnp.logical_not(self.own))(go)

        def start(self):
            self.apart(lambda: self.away.start())
            if self.own is not None:

                @pl.when(self.own)
                def _():
                    pltpu.make_async_copy(self.src, self.dst, self.rs).start()

            under_way.append(self)

        def wait(self):
            if self.recv:
                self.away.wait_recv()
            self.recv = False

        def sent(self):
            self.apart(lambda: self.away.wait_send())

    def drain():
        for item in under_way:
            item.wait()
        for item in under_way:
            item.sent()

    loads = {}
    for n, (name, src, dst) in enumerate(
        [
            ("x0", x_in.at[0], x0), ("gain", gain_in, gain), ("vw", vw_in.at[1], vw), ("q", q_in, q), ("k", k_in, k),
            ("wo1", wo_in.at[1], wo.at[1]), ("cot", cot_in, cot), ("wo0", wo_in.at[0], wo.at[0]), ("x1", x_in.at[1], xt.at[y]),
        ]
    ):
        loads[name] = pltpu.make_async_copy(src, dst, in_r.at[n])
        loads[name].start()

    barrier = pltpu.get_barrier_semaphore()

    def hello(dev):
        pl.semaphore_signal(barrier, inc=1, device_id=dev, device_id_type=MESH)

    for n in FAR_FIRST:
        hello(on_y(wrap(y + n)))
        hello(on_z(wrap(z + n)))
        hello(on_g(wrap(g + n)))

    shifts = tuple(c // 2 if c % 2 == 0 else (4 if c == 1 else 8 - c // 2) for c in range(N))
    shift = jnp.where(core == 0, g // 2, jnp.where(g == 1, 4, 8 - g // 2))
    head_here = shift == 0
    taker = on_y(wrap(y + 8 - shift))
    mirror = 7 - z
    rows32 = pl.multiple_of(32 * g, 32)
    mine = pl.ds(pl.multiple_of(HALF * near, 128), HALF)
    other = pl.ds(pl.multiple_of(HALF * (1 - near), 128), HALF)
    wo_chunk = [
        Single(wo_in.at[l, pl.ds(rows32, 32), :], wot.at[l, g], wz_s.at[l], wz_r.at[l], on_z(mirror)) for l in (0, 1)
    ]
    slice_rows = pl.ds(pl.multiple_of(32 * lax.rem(z, 4), 32), 32)
    swap_slice = Single(gvt.at[slice_rows, :], mrx, sw_s.at[0], sw_r.at[0], taker, head_here)
    taken = pl.ds(pl.multiple_of(FB * wrap(y + 8 - shift), 16), FB)
    swap_block = Single(vw_in.at[:, taken, :], vb.at[g], sw_s.at[1], sw_r.at[1], taker, head_here)
    inputs = RelayGather(x_in.at[1], xt, (xt_s, xt_r))
    squares = Gather(sq, y, (sq_s, sq_r), on_y)
    mixed = Exchange(x0p, x0a, g, (x0a_s, x0a_r), on_g)
    mixed_y = RelayGather(x0y.at[y], x0y, (x0y_s, x0y_r))
    products = Gather(mz, z, (mz_s, mz_r), on_z)
    maps = ChipGather(mt, g, (mt_s, mt_r), on_g)
    blocks = ChipGather(vb, g, (vb_s, vb_r), on_g)
    normed = Exchange(xnb, xna, z, (xn_s, xn_r), on_z)
    wo_parts = [ChipGather(wot.at[l], g, (wx_s.at[l], wx_r.at[l]), on_g) for l in (0, 1)]
    heads = [
        Gather(dvy.at[0], y, (dvy_s.at[0], dvy_r.at[0]), on_y),
        RelayGather(dvy.at[1, y], dvy.at[1], (dvy_s.at[1], dvy_r.at[1])),
    ]
    group = [
        Gather(dva.at[l], (g, z)[l], (dva_s.at[l], dva_r.at[l]), (on_g, on_z)[l]) for l in (0, 1)
    ]
    means = [Gather(mm.at[l], y, (mm_s.at[l], mm_r.at[l]), on_y) for l in (0, 1)]
    weights = [
        Exchange(dws.at[l], dwr.at[l], (z, g)[l], (dw_s.at[l], dw_r.at[l]), (on_z, on_g)[l]) for l in (0, 1)
    ]
    gains_g = Gather(gx, g, (gx_s, gx_r), on_g)
    gains_z = Gather(gz, z, (gz_s, gz_r), on_z)

    pl.semaphore_wait(barrier, 3 * (N - 1))

    wo_chunk[1].start()
    wo_chunk[0].start()
    inputs.start()
    loads["x0"].wait()
    xf = x0[...].astype(F32)
    sq[y] = jnp.broadcast_to(jnp.sum(xf * xf, axis=0, keepdims=True), (8, TOK))
    squares.start()

    loads["gain"].wait()
    loads["vw"].wait()
    for i in range(HALF // 128):
        rows = pl.ds(pl.multiple_of(HALF * near + 128 * i, 128), 128)
        part = jnp.transpose(vw[rows, :].astype(F32))
        gvt[:, 128 * i : 128 * i + 128] = (part * gain[1:2, rows]).astype(BF)
    swap_slice.start()
    swap_block.start()
    for i in range(D // 128):
        two = gain[:, 128 * i : 128 * i + 128]
        gcol[128 * i : 128 * i + 128, :] = jnp.transpose(jnp.concatenate([two, two, two, two], 0))

    wo_chunk[1].wait()
    wo_parts[1].start()
    own_rows = pl.ds(pl.multiple_of(FB * y, 32), FB)

    squares.wait()
    inv0 = lax.rsqrt(sum_of(sq)[0:1] * (1.0 / D) + 1e-6)
    dwf[...] = x0[...].astype(F32) * inv0 * gcol[own_rows, 0:1]
    for n in range(N):
        x0p[n] = jnp.concatenate([dwf[ROWS * n : ROWS * n + ROWS, :], jnp.zeros((48 - ROWS, TOK), F32)], 0).astype(BF)
    mixed.start()


    loads["q"].wait()
    loads["k"].wait()
    causal = lax.broadcasted_iota(jnp.int32, (TOK, TOK), 0) <= lax.broadcasted_iota(jnp.int32, (TOK, TOK), 1)

    def attend(l):
        for h in (0, 1):
            scores = nt(k[l], q[l, :, HD * h : HD * h + HD])
            raised = jnp.where(causal, jnp.exp(50.0 * jnp.tanh(scores * (1.0 / 600.0))), 0.0)
            probs[2 * l + h] = (raised / jnp.sum(raised, axis=0, keepdims=True)).astype(BF)

    attend(1)
    loads["wo1"].wait()
    loads["cot"].wait()
    dctx1 = nt(wo[1], cot[:, mine])
    loads["wo0"].wait()
    loads["x1"].wait()
    swap_slice.wait()
    mz[z] = nt(mrx[...], wo[0]).astype(BF)
    products.start()

    wo_chunk[0].wait()
    wo_parts[0].start()

    inputs.relay()
    wo_parts[1].pass_on()
    mixed.wait()
    for n in range(N):
        dwf[ROWS * n : ROWS * n + ROWS, :] = x0a[n].astype(F32)[0:ROWS]
    x0y[y] = dwf[...].astype(BF)
    mixed_y.start()
    wo_parts[1].wait()

    def values(l, dctx):
        return nt(probs[2 * l], dctx[0:HD]) + nt(probs[2 * l + 1], dctx[HD : 2 * HD])

    dctx1 = (dctx1 + nt(wot[1].reshape(2 * HD, HALF), cot[:, other])).astype(BF)
    dv = values(1, dctx1).astype(BF)
    dvy[1, y] = dv
    dva[1, z] = dv
    heads[1].start()
    group[1].start()
    products.wait()
    m_sum = mz[0:4].reshape(HD, 2 * HD).astype(F32) + mz[4:8].reshape(HD, 2 * HD).astype(F32)
    mt[g] = jnp.transpose(m_sum).astype(BF)
    maps.start()


    attend(0)
    wo_parts[0].pass_on()
    maps.pass_on()

    inputs.wait()
    total = jnp.zeros((1, TOK), F32)
    for b in range(N):
        xf = xt[b].astype(F32)
        total = total + jnp.sum(xf * xf, axis=0, keepdims=True)
    inv1 = lax.rsqrt(total * (1.0 / D) + 1e-6)
    total = jnp.zeros((1, TOK), F32)
    for b in range(N):
        xnb[b] = (xt[b].astype(F32) * inv1 * gcol[FB * b : FB * b + FB, 1:2]).astype(BF)
        dxn = nt(vw[FB * b : FB * b + FB, :], dvy[1, y])
        total = total + jnp.sum(dxn * xnb[b].astype(F32), axis=0, keepdims=True)
    mm[1, y] = jnp.broadcast_to(total * (1.0 / D), (8, TOK))
    means[1].start()
    normed.start()

    wo_parts[0].wait()
    wo_other = wot[0].reshape(2 * HD, HALF)
    base = nt(wo[0], cot[:, mine]) + nt(wo_other, cot[:, other])
    xt_half = [xt[0:4].reshape(HALF, TOK), xt[4:8].reshape(HALF, TOK)]
    first = near == 0
    xt_mine = jnp.where(first, xt_half[0], xt_half[1])
    xt_other = jnp.where(first, xt_half[1], xt_half[0])
    y1 = nn(wo[0], xt_mine) + nn(wo_other, xt_other)
    heads[1].relay()
    mixed_y.relay()

    maps.wait()
    swap_block.wait()
    blocks.start()
    heads[1].wait()

    def over_heads(left, l):
        total = nt(left(0), dvy[l, wrap(y + shifts[0])])
        for n in range(1, N):
            total = total + nt(left(n), dvy[l, wrap(y + shifts[n])])
        return total

    corr = over_heads(lambda n: mt[n], 1)
    means[1].wait()
    mean1 = sum_of(mm.at[1])[0:1, :]
    dctx0 = (base + inv1 * (corr - (inv1 * mean1) * y1)).astype(BF)
    dv = values(0, dctx0).astype(BF)
    dvy[0, y] = dv
    dva[0, g] = dv
    group[0].start()
    heads[0].start()
    blocks.pass_on()

    for b in range(N):

        @pl.when(y == b)
        def _():
            pad[:, 0:FB] = cot[:, FB * b : FB * b + FB].astype(F32)

    cot_blk[0:128, :] = jnp.transpose(pad[:, 0:128])
    cot_blk[128:256, :] = jnp.transpose(pad[:, 128:256])
    cot_blk[256:288, :] = jnp.transpose(pad[:, 256:384])[0:32]

    def weight_grad(l, left):
        block = nn(left(0), dva[l, 0])
        for n in range(1, N):
            block = block + nn(left(n), dva[l, n])
        dwf[...] = block * scale
        for n in range(N):
            dws[l, n, 0:ROWS, :] = dwf[ROWS * n : ROWS * n + ROWS, :]
            dws[l, n, ROWS:40, :] = jnp.zeros((40 - ROWS, HD), F32)
        weights[l].start()

    def weight_sum(l):
        weights[l].wait()
        dw_out[:, l, :] = sum_of(dwr.at[l])[0:ROWS]

    ones = jnp.ones((8, TOK), F32)

    def input_grad(l, own, inv):
        dxn = over_heads(lambda n: vb[n, l], l)
        xhat = own * inv
        row = lax.dot_general(
            ones, dxn * xhat, (((1,), (1,)), ((), ())), precision=lax.Precision.HIGHEST, preferred_element_type=F32
        )
        gx[g, l : l + 1, 0:FB] = row[0:1] * scale
        return xhat, dxn * gcol[own_rows, l : l + 1]

    gx[g] = jnp.zeros((8, 384), F32)
    blocks.wait()
    xhat, gg = input_grad(1, xt[y].astype(F32), inv1)
    cot_blk[...] = (cot_blk[...] + inv1 * (gg - xhat * mean1)).astype(BF).astype(F32)

    heads[0].wait()
    xhat, gg = input_grad(0, x0[...].astype(F32), inv0)
    gains_g.start()
    mm[0, y] = jnp.broadcast_to(jnp.sum(gg * xhat, axis=0, keepdims=True) * (1.0 / D), (8, TOK))
    means[0].start()
    mixed_y.wait()
    for b in range(N):
        dwf[...] = x0y[b].astype(F32)
        for n in range(N):
            xnf[n, ROWS * b : ROWS * b + ROWS, :] = dwf[ROWS * n : ROWS * n + ROWS, :]
    for n in range(N):
        x0w[n] = xnf[n].astype(BF)
    group[0].wait()
    weight_grad(0, lambda n: x0w[n])

    gains_g.wait()
    gz[z] = sum_of(gx)
    gains_z.start()
    normed.wait()
    group[1].wait()
    weight_grad(1, lambda n: xna[n])

    means[0].wait()
    out[...] = (cot_blk[...] + inv0 * (gg - xhat * sum_of(mm.at[0])[0:1, :])).astype(BF)

    weight_sum(1)
    weight_sum(0)
    gains_z.wait()
    gain_out[...] = sum_of(gz)[0:2, 0:FB]
    drain()


def body(grad_output, layer_input, norm_gain, queries, keys, value_weight, output_weight):
    vmem = pltpu.VMEM
    dma = pltpu.SemaphoreType.DMA
    one = [dma((N,)), dma((N,))]
    two = [dma((2, N)), dma((2, N))]
    pair = [dma((2,)), dma((2,))]
    hbm = pl.BlockSpec(memory_space=pltpu.HBM)
    out, weights, gains = pl.pallas_call(
        kernel,
        out_shape=(
            vmem((FB, TOK), BF),
            vmem((ROWS, 2, HD), F32),
            vmem((2, FB), F32),
        ),
        in_specs=[hbm] * 7,
        out_specs=[pl.BlockSpec(memory_space=vmem)] * 3,
        scratch_shapes=[
            vmem((TOK, D), BF),
            vmem((2, D), F32),
            vmem((2, TOK, 2 * HD), BF),
            vmem((2, TOK, HD), BF),
            vmem((D, HD), BF),
            vmem((2, 2 * HD, HALF), BF),
            vmem((FB, TOK), BF),
            vmem((N, FB, TOK), BF),
            vmem((N, 48, TOK), BF),
            vmem((N, 48, TOK), BF),
            vmem((N, FB, TOK), BF),
            vmem((N, FB, TOK), BF),
            vmem((D, 8), F32),
            vmem((HD, HALF), BF),
            vmem((4, TOK, TOK), BF),
            vmem((2, N, 32, HALF), BF),
            vmem((32, HALF), BF),
            vmem((N, 32, 2 * HD), BF),
            vmem((N, 2 * HD, HD), BF),
            vmem((N, 2, FB, HD), BF),
            vmem((N, FB, TOK), BF),
            vmem((N, FB, TOK), F32),
            vmem((N, FB, TOK), BF),
            vmem((2, N, TOK, HD), BF),
            vmem((2, N, TOK, HD), BF),
            vmem((N, 8, TOK), F32),
            vmem((2, N, 8, TOK), F32),
            vmem((N, 8, 384), F32),
            vmem((N, 8, 384), F32),
            vmem((FB, HD), F32),
            vmem((2, N, 40, HD), F32),
            vmem((2, N, 40, HD), F32),
            vmem((TOK, 384), F32),
            vmem((FB, TOK), F32),
        ]
        + [dma((9,))]
        + one
        + one
        + one
        + pair
        + pair
        + two
        + one
        + one
        + one
        + one
        + two
        + two
        + one
        + two
        + one
        + one
        + two,
        compiler_params=pltpu.CompilerParams(
            collective_id=0, has_side_effects=True, vmem_limit_bytes=63 * 2**20
        ),
    )(grad_output, jnp.swapaxes(layer_input, 1, 2), norm_gain, queries, keys, value_weight, output_weight)
    return jnp.swapaxes(out, 0, 1), jnp.swapaxes(weights, 0, 1), gains


def solution(mesh):
    return jax.shard_map(
        body,
        mesh=mesh,
        in_specs=(
            P(("near", "far"), None),
            P(None, ("near", "far"), "tensor"),
            P(),
            P(None, ("near", "far"), "tensor"),
            P(None, ("near", "far"), "tensor"),
            P(None, None, "tensor"),
            P(None, "tensor", "near"),
        ),
        out_specs=(
            P(("near", "far"), "tensor"),
            P(None, ("near", "far"), "tensor"),
            P(None, "tensor"),
        ),
        check_vma=False,
    )
```

```python
import math

import jax
import jax.numpy as jnp
from jax import lax
from jax.experimental import pallas as pl
from jax.experimental.pallas import tpu as pltpu
from jax.sharding import PartitionSpec as P

MESH = pl.DeviceIdType.MESH
F32 = jnp.float32
BF = jnp.bfloat16

N = 8
TOK = 128
HD = 128
FB = 288
D = 2304
HALF = 1152
ROWS = 36
FAR_FIRST = (4, 3, 5, 2, 6, 1, 7)
NEAR_FIRST = (1, 7, 2, 6, 3, 5, 4)


def nt(a, b):
    return lax.dot_general(a, b, (((1,), (1,)), ((), ())), preferred_element_type=F32)


def nn(a, b):
    return lax.dot_general(a, b, (((1,), (0,)), ((), ())), preferred_element_type=F32)


def wrap(i):
    return lax.rem(i, N)


def device(y, z, g):
    return (y, z // 4, lax.rem(z, 4) * 8 + g)


def sum_of(ref):
    total = ref[0]
    for n in range(1, N):
        total = total + ref[n]
    return total


def kernel(
    cot_in, x_in, gain_in, q_in, k_in, vw_in, wo_in,
    out, dw_out, gain_out,
    cot, gain, q, k, vw, wo, x0,
    xt, x0p, x0a, x0y, x0w, gcol, gvt, probs, wot, mrx, mz, mt, vb, xnb, xnf, xna, dvy, dva, sq, mm, gx, gz, dwf, dws, dwr, pad, cot_blk,
    in_r, xt_s, xt_r, x0a_s, x0a_r, x0y_s, x0y_r, sw_s, sw_r, wz_s, wz_r, wx_s, wx_r, mz_s, mz_r, mt_s, mt_r, vb_s, vb_r, xn_s, xn_r,
    dvy_s, dvy_r, dva_s, dva_r, sq_s, sq_r, mm_s, mm_r, gx_s, gx_r, gz_s, gz_r, dw_s, dw_r,
):
    scale = 1.0 / math.sqrt(8192.0)
    y = lax.axis_index("tensor")
    data = lax.axis_index("near") * 32 + lax.axis_index("far")
    z = data // N
    g = lax.rem(data, N)
    near = z // 4
    core = lax.rem(g, 2)
    sib = g + 1 - 2 * core

    def on_y(i):
        return device(i, z, g)

    def on_z(i):
        return device(y, i, g)

    def on_g(i):
        return device(y, z, i)

    def copy(src, dst, ss, rs, dev):
        return pltpu.make_async_remote_copy(
            src_ref=src, dst_ref=dst, send_sem=ss, recv_sem=rs, device_id=dev, device_id_type=MESH
        )

    under_way = []

    class Gather:
        def __init__(self, buf, me, sems, dev):
            self.buf, self.me, (self.ss, self.rs), self.dev = buf, me, sems, dev

        def one(self, n, slot, dev):
            return copy(self.buf.at[slot], self.buf.at[slot], self.ss.at[n], self.rs.at[slot], dev)

        def start(self):
            for n in FAR_FIRST:
                self.one(n, self.me, self.dev(wrap(self.me + n))).start()
            under_way.append(self)

        def arrived(self, n):
            slot = wrap(self.me + n)
            self.one(n, slot, self.dev(slot)).wait_recv()

        def wait(self):
            for n in NEAR_FIRST:
                self.arrived(n)
            self.wait = lambda: None

        def sent(self):
            for n in range(1, N):
                self.one(n, self.me, self.dev(wrap(self.me + n))).wait_send()

    class ChipGather(Gather):
        def start(self):
            for n in (4, 2, 6):
                self.one(n, g, on_g(wrap(g + n))).start()
            self.one(1, g, on_g(sib)).start()
            under_way.append(self)

        def pass_on(self):
            for n in (2, 6, 4):
                slot = wrap(g + n)
                self.one(n, slot, on_g(slot)).wait_recv()
                self.one(n + 1, slot, on_g(sib)).start()
            self.pass_on = lambda: None

        def wait(self):
            self.pass_on()
            for n in (0, 2, 6, 4):
                slot = wrap(sib + n)
                self.one(1, slot, on_g(sib)).wait_recv()
            self.wait = lambda: None

        def sent(self):
            for n in range(1, N):
                self.one(n, g, on_g(sib)).wait_send()

    class Exchange(Gather):
        def __init__(self, src, buf, me, sems, dev):
            super().__init__(buf, me, sems, dev)
            self.src = src

        def to(self, n):
            i = wrap(self.me + n)
            return copy(self.src.at[i], self.buf.at[self.me], self.ss.at[n], self.rs.at[self.me], self.dev(i))

        def start(self):
            for n in FAR_FIRST:
                self.to(n).start()
            pltpu.make_async_copy(self.src.at[self.me], self.buf.at[self.me], self.rs.at[self.me]).start()
            under_way.append(self)

        def wait(self):
            for n in (0,) + NEAR_FIRST:
                self.arrived(n)
            self.wait = lambda: None

        def sent(self):
            for n in range(1, N):
                self.to(n).wait_send()

    class RelayGather(Gather):
        def __init__(self, src, buf, sems):
            super().__init__(buf, y, sems, on_y)
            self.src = src

        def own(self, n):
            return copy(self.src, self.buf.at[y], self.ss.at[n], self.rs.at[y], on_y(wrap(y + n)))

        def start(self):
            for n in (2, 6, 1, 7):
                self.own(n).start()
            under_way.append(self)

        def on(self, m):
            sign = 1 - 2 * lax.rem(y, 2)
            source, target = ((6, 1), (2, 7), (8 - 2 * sign, 8 + 2 * sign))[m]
            slot = wrap(y + source)
            return copy(
                self.buf.at[slot], self.buf.at[slot], self.ss.at[3 + m], self.rs.at[slot], on_y(wrap(y + target))
            )

        def relay(self):
            for n in (2, 6):
                self.arrived(n)
            for m in (2, 0, 1):
                self.on(m).start()
            self.relay = lambda: None

        def arrived(self, n):
            slot = wrap(y + n)
            self.one(0, slot, on_y(slot)).wait_recv()

        def wait(self):
            self.relay()
            for n in (1, 7, 3, 5, 4):
                self.arrived(n)
            self.wait = lambda: None

        def sent(self):
            for n in (2, 6, 1, 7):
                self.own(n).wait_send()
            for m in (0, 1, 2):
                self.on(m).wait_send()

    class Single:
        def __init__(self, src, dst, ss, rs, dev, own=None, recv=True):
            self.src, self.dst, self.rs, self.own, self.recv = src, dst, rs, own, recv
            self.away = copy(src, dst, ss, rs, dev)

        def apart(self, go):
            if self.own is None:
                go()
            else:
                pl.when(jnp.logical_not(self.own))(go)

        def start(self):
            self.apart(lambda: self.away.start())
            if self.own is not None:

                @pl.when(self.own)
                def _():
                    pltpu.make_async_copy(self.src, self.dst, self.rs).start()

            under_way.append(self)

        def wait(self):
            if self.recv:
                self.away.wait_recv()
            self.recv = False

        def sent(self):
            self.apart(lambda: self.away.wait_send())

    def drain():
        for item in under_way:
            item.wait()
        for item in under_way:
            item.sent()

    barrier = pltpu.get_barrier_semaphore()

    def hello(dev):
        pl.semaphore_signal(barrier, inc=1, device_id=dev, device_id_type=MESH)

    for n in FAR_FIRST:
        hello(on_y(wrap(y + n)))
        hello(on_z(wrap(z + n)))
        hello(on_g(wrap(g + n)))

    loads = {}
    for n, (name, src, dst) in enumerate(
        [
            ("x0", x_in.at[0], x0), ("gain", gain_in, gain), ("vw", vw_in.at[1], vw), ("q", q_in, q), ("k", k_in, k),
            ("wo1", wo_in.at[1], wo.at[1]), ("cot", cot_in, cot), ("wo0", wo_in.at[0], wo.at[0]), ("x1", x_in.at[1], xt.at[y]),
        ]
    ):
        loads[name] = pltpu.make_async_copy(src, dst, in_r.at[n])
        loads[name].start()

    shifts = tuple(c // 2 if c % 2 == 0 else (4 if c == 1 else 8 - c // 2) for c in range(N))
    shift = jnp.where(core == 0, g // 2, jnp.where(g == 1, 4, 8 - g // 2))
    head_here = shift == 0
    taker = on_y(wrap(y + 8 - shift))
    mirror = 7 - z
    rows32 = pl.multiple_of(32 * g, 32)
    mine = pl.ds(pl.multiple_of(HALF * near, 128), HALF)
    other = pl.ds(pl.multiple_of(HALF * (1 - near), 128), HALF)
    wo_chunk = [
        Single(wo_in.at[l, pl.ds(rows32, 32), :], wot.at[l, g], wz_s.at[l], wz_r.at[l], on_z(mirror)) for l in (0, 1)
    ]
    slice_rows = pl.ds(pl.multiple_of(32 * lax.rem(z, 4), 32), 32)
    swap_slice = Single(gvt.at[slice_rows, :], mrx, sw_s.at[0], sw_r.at[0], taker, head_here)
    taken = pl.ds(pl.multiple_of(FB * wrap(y + 8 - shift), 16), FB)
    swap_block = Single(vw_in.at[:, taken, :], vb.at[g], sw_s.at[1], sw_r.at[1], taker, head_here)
    inputs = RelayGather(x_in.at[1], xt, (xt_s, xt_r))
    squares = Gather(sq, y, (sq_s, sq_r), on_y)
    mixed = Exchange(x0p, x0a, g, (x0a_s, x0a_r), on_g)
    mixed_y = RelayGather(x0y.at[y], x0y, (x0y_s, x0y_r))
    products = Gather(mz, z, (mz_s, mz_r), on_z)
    maps = ChipGather(mt, g, (mt_s, mt_r), on_g)
    blocks = ChipGather(vb, g, (vb_s, vb_r), on_g)
    normed = Exchange(xnb, xna, z, (xn_s, xn_r), on_z)
    wo_parts = [ChipGather(wot.at[l], g, (wx_s.at[l], wx_r.at[l]), on_g) for l in (0, 1)]
    heads = [
        Gather(dvy.at[0], y, (dvy_s.at[0], dvy_r.at[0]), on_y),
        RelayGather(dvy.at[1, y], dvy.at[1], (dvy_s.at[1], dvy_r.at[1])),
    ]
    group = [
        Gather(dva.at[l], (g, z)[l], (dva_s.at[l], dva_r.at[l]), (on_g, on_z)[l]) for l in (0, 1)
    ]
    means = [Gather(mm.at[l], y, (mm_s.at[l], mm_r.at[l]), on_y) for l in (0, 1)]
    weights = [
        Exchange(dws.at[l], dwr.at[l], (z, g)[l], (dw_s.at[l], dw_r.at[l]), (on_z, on_g)[l]) for l in (0, 1)
    ]
    gains_g = Gather(gx, g, (gx_s, gx_r), on_g)
    gains_z = Gather(gz, z, (gz_s, gz_r), on_z)

    pl.semaphore_wait(barrier, 3 * (N - 1))

    wo_chunk[1].start()
    wo_chunk[0].start()
    inputs.start()
    loads["x0"].wait()
    xf = x0[...].astype(F32)
    sq[y] = jnp.broadcast_to(jnp.sum(xf * xf, axis=0, keepdims=True), (8, TOK))
    squares.start()

    loads["gain"].wait()
    loads["vw"].wait()
    for i in range(HALF // 128):
        rows = pl.ds(pl.multiple_of(HALF * near + 128 * i, 128), 128)
        part = jnp.transpose(vw[rows, :].astype(F32))
        gvt[:, 128 * i : 128 * i + 128] = (part * gain[1:2, rows]).astype(BF)
    swap_slice.start()
    swap_block.start()
    for i in range(D // 128):
        two = gain[:, 128 * i : 128 * i + 128]
        gcol[128 * i : 128 * i + 128, :] = jnp.transpose(jnp.concatenate([two, two, two, two], 0))

    wo_chunk[1].wait()
    wo_parts[1].start()
    own_rows = pl.ds(pl.multiple_of(FB * y, 32), FB)

    squares.wait()
    inv0 = lax.rsqrt(sum_of(sq)[0:1] * (1.0 / D) + 1e-6)
    dwf[...] = x0[...].astype(F32) * inv0 * gcol[own_rows, 0:1]
    for n in range(N):
        x0p[n] = jnp.concatenate([dwf[ROWS * n : ROWS * n + ROWS, :], jnp.zeros((48 - ROWS, TOK), F32)], 0).astype(BF)
    mixed.start()


    loads["q"].wait()
    loads["k"].wait()
    causal = lax.broadcasted_iota(jnp.int32, (TOK, TOK), 0) <= lax.broadcasted_iota(jnp.int32, (TOK, TOK), 1)

    def attend(l):
        for h in (0, 1):
            scores = nt(k[l], q[l, :, HD * h : HD * h + HD])
            raised = jnp.where(causal, jnp.exp(50.0 * jnp.tanh(scores * (1.0 / 600.0))), 0.0)
            probs[2 * l + h] = (raised / jnp.sum(raised, axis=0, keepdims=True)).astype(BF)

    attend(1)
    loads["wo1"].wait()
    loads["cot"].wait()
    dctx1 = nt(wo[1], cot[:, mine])
    loads["wo0"].wait()
    loads["x1"].wait()
    swap_slice.wait()
    mz[z] = nt(mrx[...], wo[0]).astype(BF)
    products.start()

    wo_chunk[0].wait()
    wo_parts[0].start()

    inputs.relay()
    wo_parts[1].pass_on()
    mixed.wait()
    for n in range(N):
        dwf[ROWS * n : ROWS * n + ROWS, :] = x0a[n].astype(F32)[0:ROWS]
    x0y[y] = dwf[...].astype(BF)
    mixed_y.start()
    wo_parts[1].wait()

    def values(l, dctx):
        return nt(probs[2 * l], dctx[0:HD]) + nt(probs[2 * l + 1], dctx[HD : 2 * HD])

    dctx1 = (dctx1 + nt(wot[1].reshape(2 * HD, HALF), cot[:, other])).astype(BF)
    dv = values(1, dctx1).astype(BF)
    dvy[1, y] = dv
    dva[1, z] = dv
    heads[1].start()
    group[1].start()
    products.wait()
    m_sum = mz[0:4].reshape(HD, 2 * HD).astype(F32) + mz[4:8].reshape(HD, 2 * HD).astype(F32)
    mt[g] = jnp.transpose(m_sum).astype(BF)
    maps.start()


    attend(0)
    wo_parts[0].pass_on()
    maps.pass_on()

    inputs.wait()
    total = jnp.zeros((1, TOK), F32)
    for b in range(N):
        xf = xt[b].astype(F32)
        total = total + jnp.sum(xf * xf, axis=0, keepdims=True)
    inv1 = lax.rsqrt(total * (1.0 / D) + 1e-6)
    total = jnp.zeros((1, TOK), F32)
    for b in range(N):
        xnb[b] = (xt[b].astype(F32) * inv1 * gcol[FB * b : FB * b + FB, 1:2]).astype(BF)
        dxn = nt(vw[FB * b : FB * b + FB, :], dvy[1, y])
        total = total + jnp.sum(dxn * xnb[b].astype(F32), axis=0, keepdims=True)
    mm[1, y] = jnp.broadcast_to(total * (1.0 / D), (8, TOK))
    means[1].start()
    heads[1].relay()
    normed.start()

    wo_parts[0].wait()
    wo_other = wot[0].reshape(2 * HD, HALF)
    base = nt(wo[0], cot[:, mine]) + nt(wo_other, cot[:, other])
    xt_half = [xt[0:4].reshape(HALF, TOK), xt[4:8].reshape(HALF, TOK)]
    first = near == 0
    xt_mine = jnp.where(first, xt_half[0], xt_half[1])
    xt_other = jnp.where(first, xt_half[1], xt_half[0])
    y1 = nn(wo[0], xt_mine) + nn(wo_other, xt_other)
    mixed_y.relay()

    maps.wait()
    swap_block.wait()
    blocks.start()
    heads[1].wait()

    def over_heads(left, l):
        total = nt(left(0), dvy[l, wrap(y + shifts[0])])
        for n in range(1, N):
            total = total + nt(left(n), dvy[l, wrap(y + shifts[n])])
        return total

    corr = over_heads(lambda n: mt[n], 1)
    means[1].wait()
    mean1 = sum_of(mm.at[1])[0:1, :]
    dctx0 = (base + inv1 * (corr - (inv1 * mean1) * y1)).astype(BF)
    dv = values(0, dctx0).astype(BF)
    dvy[0, y] = dv
    dva[0, g] = dv
    heads[0].start()
    group[0].start()
    blocks.pass_on()

    for b in range(N):

        @pl.when(y == b)
        def _():
            pad[:, 0:FB] = cot[:, FB * b : FB * b + FB].astype(F32)

    cot_blk[0:128, :] = jnp.transpose(pad[:, 0:128])
    cot_blk[128:256, :] = jnp.transpose(pad[:, 128:256])
    cot_blk[256:288, :] = jnp.transpose(pad[:, 256:384])[0:32]

    def weight_grad(l, left):
        block = nn(left(0), dva[l, 0])
        for n in range(1, N):
            block = block + nn(left(n), dva[l, n])
        dwf[...] = block * scale
        for n in range(N):
            dws[l, n, 0:ROWS, :] = dwf[ROWS * n : ROWS * n + ROWS, :]
            dws[l, n, ROWS:40, :] = jnp.zeros((40 - ROWS, HD), F32)
        weights[l].start()

    def weight_sum(l):
        weights[l].wait()
        dw_out[:, l, :] = sum_of(dwr.at[l])[0:ROWS]

    ones = jnp.ones((8, TOK), F32)

    def input_grad(l, own, inv):
        dxn = over_heads(lambda n: vb[n, l], l)
        xhat = own * inv
        row = lax.dot_general(
            ones, dxn * xhat, (((1,), (1,)), ((), ())), precision=lax.Precision.HIGHEST, preferred_element_type=F32
        )
        gx[g, l : l + 1, 0:FB] = row[0:1] * scale
        return xhat, dxn * gcol[own_rows, l : l + 1]

    gx[g] = jnp.zeros((2, 384), F32)
    blocks.wait()
    xhat, gg = input_grad(1, xt[y].astype(F32), inv1)
    cot_blk[...] = (cot_blk[...] + inv1 * (gg - xhat * mean1)).astype(BF).astype(F32)

    heads[0].wait()
    xhat, gg = input_grad(0, x0[...].astype(F32), inv0)
    gains_g.start()
    mm[0, y] = jnp.broadcast_to(jnp.sum(gg * xhat, axis=0, keepdims=True) * (1.0 / D), (8, TOK))
    means[0].start()
    mixed_y.wait()
    for b in range(N):
        dwf[...] = x0y[b].astype(F32)
        for n in range(N):
            xnf[n, ROWS * b : ROWS * b + ROWS, :] = dwf[ROWS * n : ROWS * n + ROWS, :]
    for n in range(N):
        x0w[n] = xnf[n].astype(BF)
    group[0].wait()
    weight_grad(0, lambda n: x0w[n])

    gains_g.wait()
    gz[z] = sum_of(gx)
    gains_z.start()
    normed.wait()
    group[1].wait()
    weight_grad(1, lambda n: xna[n])

    means[0].wait()
    out[...] = (cot_blk[...] + inv0 * (gg - xhat * sum_of(mm.at[0])[0:1, :])).astype(BF)

    weight_sum(1)
    weight_sum(0)
    gains_z.wait()
    gain_out[...] = sum_of(gz)[0:2, 0:FB]
    drain()


def body(grad_output, layer_input, norm_gain, queries, keys, value_weight, output_weight):
    vmem = pltpu.VMEM
    dma = pltpu.SemaphoreType.DMA
    one = [dma((N,)), dma((N,))]
    two = [dma((2, N)), dma((2, N))]
    pair = [dma((2,)), dma((2,))]
    hbm = pl.BlockSpec(memory_space=pltpu.HBM)
    out, weights, gains = pl.pallas_call(
        kernel,
        out_shape=(
            vmem((FB, TOK), BF),
            vmem((ROWS, 2, HD), F32),
            vmem((2, FB), F32),
        ),
        in_specs=[hbm] * 7,
        out_specs=[pl.BlockSpec(memory_space=vmem)] * 3,
        scratch_shapes=[
            vmem((TOK, D), BF),
            vmem((2, D), F32),
            vmem((2, TOK, 2 * HD), BF),
            vmem((2, TOK, HD), BF),
            vmem((D, HD), BF),
            vmem((2, 2 * HD, HALF), BF),
            vmem((FB, TOK), BF),
            vmem((N, FB, TOK), BF),
            vmem((N, 48, TOK), BF),
            vmem((N, 48, TOK), BF),
            vmem((N, FB, TOK), BF),
            vmem((N, FB, TOK), BF),
            vmem((D, 8), F32),
            vmem((HD, HALF), BF),
            vmem((4, TOK, TOK), BF),
            vmem((2, N, 32, HALF), BF),
            vmem((32, HALF), BF),
            vmem((N, 32, 2 * HD), BF),
            vmem((N, 2 * HD, HD), BF),
            vmem((N, 2, FB, HD), BF),
            vmem((N, FB, TOK), BF),
            vmem((N, FB, TOK), F32),
            vmem((N, FB, TOK), BF),
            vmem((2, N, TOK, HD), BF),
            vmem((2, N, TOK, HD), BF),
            vmem((N, 8, TOK), F32),
            vmem((2, N, 8, TOK), F32),
            vmem((N, 2, 384), F32),
            vmem((N, 2, 384), F32),
            vmem((FB, HD), F32),
            vmem((2, N, 40, HD), F32),
            vmem((2, N, 40, HD), F32),
            vmem((TOK, 384), F32),
            vmem((FB, TOK), F32),
        ]
        + [dma((9,))]
        + one
        + one
        + one
        + pair
        + pair
        + two
        + one
        + one
        + one
        + one
        + two
        + two
        + one
        + two
        + one
        + one
        + two,
        compiler_params=pltpu.CompilerParams(
            collective_id=0, has_side_effects=True, vmem_limit_bytes=63 * 2**20
        ),
    )(grad_output, jnp.swapaxes(layer_input, 1, 2), norm_gain, queries, keys, value_weight, output_weight)
    return jnp.swapaxes(out, 0, 1), jnp.swapaxes(weights, 0, 1), gains


def solution(mesh):
    return jax.shard_map(
        body,
        mesh=mesh,
        in_specs=(
            P(("near", "far"), None),
            P(None, ("near", "far"), "tensor"),
            P(),
            P(None, ("near", "far"), "tensor"),
            P(None, ("near", "far"), "tensor"),
            P(None, None, "tensor"),
            P(None, "tensor", "near"),
        ),
        out_specs=(
            P(("near", "far"), "tensor"),
            P(None, ("near", "far"), "tensor"),
            P(None, "tensor"),
        ),
        check_vma=False,
    )
```
